32 devices in a mesh: dp: 4 (over z), mp: 4 (over y, x), group: 2 (over core).
Axes of the slice: x: 2, y: 2, z: 4, core: 2. Of those that a mesh axis runs over, the one named last changes fastest.
Arguments:
- hidden: bfloat16 [512, 8192], P('dp', 'mp'), may hold values from -6 to 6
- neighbour_ids: int32 [8, 2, 128], P('dp', 'group'), may hold values from 0 to 65535, as said below
- counts: int32 [8], P('dp'), may hold values from 0 to 2
- embed_table: bfloat16 [65536, 8192], P(('dp', 'group'), 'mp'), may hold values from -6 to 6
- w_query: bfloat16 [8192, 4096], P('group', 'mp'), may hold values from -0.0625 to 0.0625
- w_key: bfloat16 [8192, 4096], P('group', 'mp'), may hold values from -0.0625 to 0.0625
- w_value: bfloat16 [8192, 4096], P('group', 'mp'), may hold values from -0.0625 to 0.0625
- w_out: bfloat16 [4096, 8192], P('mp', 'group'), may hold values from -0.09375 to 0.09375
- grad_out: bfloat16 [512, 8192], P('dp', 'mp'), may hold values from -6 to 6
Outputs:
- output: float32 [512, 8192], P('dp', 'mp')
- grad_hidden: float32 [512, 8192], P('dp', 'mp')
- grad_neighbours: float32 [8, 2, 128, 8192], P('dp', 'group', None, 'mp')
The draws below stay inside these ranges and needn't reach their ends.
Inputs may be any that keep to these rules, and one draw needn't show every extreme that they name: `neighbour_ids`: token ids of the retrieved neighbours; the ids are split into 8 owners of 8192 consecutive ids each; of the 256 ids of one window's neighbour k (blocks of one window, one k), at most 64 belong to one owner, and exactly 64 belong to some owner. neighbours k < counts[c] of block c are used, the others are masked.
All inputs are finite; a program needn't handle non-finite values.
Results may differ from the reference program's by a relative error of at most 0.019.
Values may be sent and summed in bfloat16 or wider, within the bound.
No kernel may reach another device: no remote copies, remote signals or barrier semaphores. Data moves between devices by JAX's collectives and lax.ppermute only.
A program may use at most 256 MiB of HBM per device.

```python
import math
import jax
import jax.numpy as jnp
from jax import lax

D = 8192
HEADS = 32
HD = 128
BLOCK = 64
RET = 128
NEIGH = 2
VOCAB = 65536
TOK_DEV = 128
HM = 8
BLK_DEV = 2
SEQS = 4
TOKENS = 512
BLOCKS = 8
CAP = 64
N_DP = 4
N_MP = 4
N_GROUP = 2


def draw_neighbour_ids(key, part):
    owners = N_DP * N_GROUP
    slots = BLK_DEV * RET
    rows_per = VOCAB // owners
    key_perm = jax.random.fold_in(key, 11)
    key_order = jax.random.fold_in(key, 12)
    key_offset = jax.random.fold_in(key, 13)
    key_row_a = jax.random.fold_in(key, 14)
    key_row_b = jax.random.fold_in(key, 15)
    owner_perm = jax.vmap(lambda k: jax.random.permutation(k, owners))(jax.random.split(key_perm, owners))
    slot_order = jax.vmap(lambda k: jax.random.permutation(k, slots))(jax.random.split(key_order, owners))
    offsets = jax.random.randint(key_offset, (owners, 1), 0, owners - 1)
    slot_index = jnp.arange(slots, dtype=jnp.int32)[None, :]
    later = 1 + (slot_index - CAP + offsets) % (owners - 1)
    rank = jnp.where(slot_index < CAP, 0, later).astype(jnp.int32)
    owner_drawn = jnp.take_along_axis(owner_perm.astype(jnp.int32), rank, 1)
    owner_mixed = jnp.take_along_axis(owner_drawn, slot_order.astype(jnp.int32), 1)
    row_a = jax.random.randint(key_row_a, (owners, slots), 0, rows_per)
    row_b = jax.random.randint(key_row_b, (owners, slots), 0, rows_per)
    ids = owner_mixed * rows_per + jnp.minimum(row_a, row_b)
    ids = ids.reshape(N_DP, N_GROUP, BLK_DEV, RET)
    ids = jnp.transpose(ids, (0, 2, 1, 3)).reshape(BLOCKS, NEIGH, RET)
    return ids.astype(jnp.int32)


def set_ends(drawn, rng, low, largest):
    spot = [jax.random.randint(jax.random.fold_in(rng, axis), (), 0, length) for axis, length in enumerate(drawn.shape)]
    longest = drawn.shape.index(max(drawn.shape))
    next_to = spot[:longest] + [(spot[longest] + 1) % drawn.shape[longest]] + spot[longest + 1:]
    return drawn.at[tuple(spot)].set(low).at[tuple(next_to)].set(largest)


def block_levels(rng, shape, cuts, smallest, top_value):
    gain, own = 1.0, jax.random.fold_in(rng, 6)
    for position, parts in cuts:
        heights = jnp.exp(jax.random.uniform(jax.random.fold_in(own, position), (parts,), jnp.float32, smallest / len(cuts), top_value / len(cuts)))
        gain = gain * jnp.repeat(heights, shape[position] // parts).reshape([-1 if axis == position else 1 for axis in range(len(shape))])
    return gain


def centred(stream_key, dims, scale, limit, cuts=(), kind=jnp.bfloat16):
    array = jax.random.normal(stream_key, dims, jnp.float32) * scale
    if len(cuts) > 0:
        array = block_levels(stream_key, dims, cuts, -0.22, 0.18) * array
    return jnp.clip(array, min=-limit, max=limit).astype(kind)


def setup_inputs(seed: int = 0) -> dict:
    key_of = jax.random.split(jax.random.key(seed), 10)
    return {
        "hidden": centred(key_of[0], (TOKENS, D), 1.0, 6.0, ((0, 4), (1, 4))),
        "neighbour_ids": draw_neighbour_ids(jax.random.fold_in(key_of[9], 71), 0),
        "counts": set_ends(jax.random.randint(key_of[2], (BLOCKS,), 0, NEIGH + 1), jax.random.fold_in(key_of[2], 1), 0, NEIGH).astype(jnp.int32),
        "embed_table": centred(key_of[3], (VOCAB, D), 1.0, 6.0, ((0, 8), (1, 4))),
        "w_query": centred(key_of[4], (D, HEADS * HD), D ** -0.5, 0.0625, ((0, 2), (1, 4))),
        "w_key": centred(key_of[5], (D, HEADS * HD), D ** -0.5, 0.0625, ((0, 2), (1, 4))),
        "w_value": centred(key_of[6], (D, HEADS * HD), D ** -0.5, 0.0625, ((0, 2), (1, 4))),
        "w_out": centred(key_of[7], (HEADS * HD, D), (HEADS * HD) ** -0.5, 0.09375, ((0, 4), (1, 2))),
        "grad_out": centred(key_of[8], (TOKENS, D), 1.0, 6.0, ((0, 4), (1, 4))),
    }


def rounded(value):
    return lax.optimization_barrier(value.astype(jnp.bfloat16)).astype(jnp.float32)

def contract(left, right):
    return lax.dot_general(left, right, (((1,), (1,)), ((), ())), preferred_element_type=jnp.float32)

def window_ahead(rows, tail_rows):
    shaped = rows.reshape(SEQS, TOK_DEV, rows.shape[1])
    padding = jnp.zeros((SEQS, tail_rows, rows.shape[1]), rows.dtype)
    return jnp.concatenate([shaped[:, tail_rows:], padding], 1).reshape(TOKENS, rows.shape[1])

def window_back(rows, tail_rows):
    shaped = rows.reshape(SEQS, TOK_DEV, rows.shape[1])
    padding = jnp.zeros((SEQS, tail_rows, rows.shape[1]), rows.dtype)
    return jnp.concatenate([padding, shaped[:, :TOK_DEV - tail_rows]], 1).reshape(TOKENS, rows.shape[1])

def reference(hidden, neighbour_ids, counts, embed_table, w_query, w_key, w_value, w_out, grad_out):
    inv_root = 1.0 / math.sqrt(HD)
    tail_rows = BLOCK - 1
    width = HEADS * HD
    group_cols = HM * HD
    neighbours = embed_table[neighbour_ids.reshape(-1)]
    keys = jnp.dot(neighbours, w_key, preferred_element_type=jnp.float32).astype(jnp.bfloat16)
    values = jnp.dot(neighbours, w_value, preferred_element_type=jnp.float32).astype(jnp.bfloat16)
    key_block = keys.reshape(BLOCKS, NEIGH * RET, HEADS, HD).astype(jnp.float32)
    value_block = values.reshape(BLOCKS, NEIGH * RET, HEADS, HD).astype(jnp.float32)
    query_rows = window_ahead(hidden, tail_rows)
    query = jnp.dot(query_rows, w_query, preferred_element_type=jnp.float32).astype(jnp.bfloat16)
    query_block = query.reshape(BLOCKS, BLOCK, HEADS, HD).astype(jnp.float32)
    slot_of = jnp.arange(NEIGH * RET, dtype=jnp.int32) // RET
    live = (slot_of[None, :] < counts[:, None]).astype(jnp.float32)
    scores = jnp.einsum('cqhd,ckhd->chqk', query_block, key_block) * inv_root
    weights = jnp.exp(scores) * live[:, None, None, :]
    total = 1.0 + lax.optimization_barrier(jnp.sum(weights, -1))
    numer = jnp.einsum('chqk,ckhd->cqhd', rounded(weights), value_block)
    attn = numer / jnp.transpose(total, (0, 2, 1))[..., None]
    attn_bf = attn.reshape(TOKENS, width).astype(jnp.bfloat16)
    out_rows = jnp.zeros((TOKENS, D), jnp.float32)
    for group_index in range(N_MP):
        lo_col = group_index * group_cols
        part = jnp.dot(attn_bf[:, lo_col:lo_col + group_cols], w_out[lo_col:lo_col + group_cols], preferred_element_type=jnp.float32)
        out_rows = out_rows + rounded(part)
    output = window_back(out_rows, tail_rows)
    grad_rows = window_ahead(grad_out, tail_rows)
    d_attn = contract(grad_rows, w_out).astype(jnp.bfloat16)
    d_block = d_attn.reshape(BLOCKS, BLOCK, HEADS, HD).astype(jnp.float32)
    prob = weights / total[..., None]
    d_prob = jnp.einsum('cqhd,ckhd->chqk', d_block, value_block)
    delta = lax.optimization_barrier(jnp.sum(d_block * attn, -1))
    d_score = rounded(prob * (d_prob - jnp.transpose(delta, (0, 2, 1))[..., None]))
    d_query = (jnp.einsum('chqk,ckhd->cqhd', d_score, key_block) * inv_root).astype(jnp.bfloat16).reshape(TOKENS, width)
    d_keys = (jnp.einsum('chqk,cqhd->ckhd', d_score, query_block) * inv_root).astype(jnp.bfloat16).reshape(BLOCKS * NEIGH * RET, width)
    d_values = jnp.einsum('chqk,cqhd->ckhd', rounded(prob), d_block).astype(jnp.bfloat16).reshape(BLOCKS * NEIGH * RET, width)
    hid_rows = jnp.zeros((TOKENS, D), jnp.float32)
    neigh_rows = jnp.zeros((BLOCKS * NEIGH * RET, D), jnp.float32)
    for group_index in range(N_MP):
        lo_col = group_index * group_cols
        hi_col = lo_col + group_cols
        hid_rows = hid_rows + rounded(contract(d_query[:, lo_col:hi_col], w_query[:, lo_col:hi_col]))
        neigh_part = contract(d_keys[:, lo_col:hi_col], w_key[:, lo_col:hi_col]) + contract(d_values[:, lo_col:hi_col], w_value[:, lo_col:hi_col])
        neigh_rows = neigh_rows + rounded(neigh_part)
    grad_hidden = window_back(hid_rows, tail_rows)
    grad_neighbours = neigh_rows.reshape(BLOCKS, NEIGH, RET, D)
    return (output, grad_hidden, grad_neighbours)
```

```python
import math

import jax
import jax.numpy as jnp
from jax import lax
from jax.sharding import PartitionSpec as P

HD = 128
BLOCK = 64
RET = 128
CAP = 64
AXES = ("dp", "mp", "group")


def contract(left, right):
    return lax.dot_general(
        left, right, (((1,), (1,)), ((), ())), preferred_element_type=jnp.float32
    )


def times(left, right):
    return jnp.dot(left, right, preferred_element_type=jnp.float32)


def from_xor(pieces, mask):
    count = pieces.shape[0]
    step = 1
    while step < count:
        split = pieces.reshape(count // (2 * step), 2, step, *pieces.shape[1:])
        swapped = jnp.concatenate([split[:, 1:], split[:, :1]], 1).reshape(pieces.shape)
        pieces = jnp.where((mask & step) != 0, swapped, pieces)
        step *= 2
    return pieces


def per_device(
    hidden, neighbour_ids, counts, embed_table, w_query, w_key, w_value, w_out, grad_out
):
    n_dp, n_mp, n_group = (lax.axis_size(name) for name in AXES)
    n_half = n_mp // n_group
    tail_rows = BLOCK - 1
    rows_here = hidden.shape[0]
    cols_here = hidden.shape[1]
    width = w_query.shape[1]
    heads_here = width // HD
    part = width // n_group
    part_heads = heads_here // n_group
    inv_root = 1.0 / math.sqrt(HD)
    block_rows = embed_table.shape[0]
    at_d, at_m, at_g = (lax.axis_index(name) for name in AXES)
    at_y, at_x = at_m // n_half, at_m % n_half

    def move(array, target):
        pairs = []
        for d in range(n_dp):
            for m in range(n_mp):
                for g in range(n_group):
                    to_d, to_m, to_g = target(d, m, g)
                    here = (d * n_mp + m) * n_group + g
                    pairs.append((here, (to_d * n_mp + to_m) * n_group + to_g))
        return lax.ppermute(array, AXES, pairs)

    def to_owner(step_d, step_g):
        return lambda d, m, g: (d ^ step_d, m, g ^ step_g)

    def to_chips(a, b):
        return lambda d, m, g: (d, (g ^ b) * n_half + ((m % n_half) ^ a), m // n_half)

    def to_columns(a, b):
        return lambda d, m, g: (d, g * n_half + ((m % n_half) ^ a), (m // n_half) ^ b)

    def other_core(array):
        return move(array, lambda d, m, g: (d, m, g ^ 1))

    def halves(array):
        first, second = array[:, :part], array[:, part:]
        return jnp.where(at_g == 0, first, second), jnp.where(at_g == 0, second, first)

    flat_ids = neighbour_ids.reshape(-1)
    slots = flat_ids.shape[0]
    pair_ids = jnp.stack([flat_ids, other_core(flat_ids)])
    every_id = [pair_ids]
    for step in range(1, n_dp):
        every_id.append(move(pair_ids, to_owner(step, 0)))
    every_id = jnp.stack(every_id)
    owner = at_d * n_group + at_g
    local_ids = every_id - owner * block_rows
    inside = (local_ids >= 0) & (local_ids < block_rows)
    before = jnp.triu(jnp.ones((slots, slots), jnp.bfloat16), 1)
    rank = times(inside.astype(jnp.bfloat16).reshape(-1, slots), before)
    rank = rank.reshape(inside.shape).astype(jnp.int32)
    slot_of = jnp.arange(CAP, dtype=jnp.int32)
    chosen = inside[:, :, None, :] & (rank[:, :, None, :] == slot_of[:, None])
    wanted = jnp.sum(jnp.where(chosen, local_ids[:, :, None, :], 0), -1)

    received = {}
    for step_d in reversed(range(n_dp)):
        for step_g in range(n_group):
            rows = embed_table.at[wanted[step_d, step_g]].get(mode="promise_in_bounds")
            if (step_d, step_g) != (0, 0):
                rows = move(rows, to_owner(step_d, step_g))
            received[step_d, step_g] = rows
    packets = [(d, g) for d in range(n_dp) for g in range(n_group)]
    own_owner = flat_ids // block_rows
    same = own_owner[:, None] == own_owner[None, :]
    earlier = jnp.arange(slots)[None, :] < jnp.arange(slots)[:, None]
    own_rank = jnp.sum((same & earlier).astype(jnp.int32), -1)
    sender = jnp.stack([(at_d ^ d) * n_group + (at_g ^ g) for d, g in packets])
    place = (own_owner[:, None, None] == sender[None, :, None]) & (
        own_rank[:, None, None] == slot_of[None, None, :]
    )
    place = place.astype(jnp.bfloat16).reshape(slots, -1)
    neighbours = times(place, jnp.concatenate([received[p] for p in packets], 0))
    neighbours = neighbours.astype(jnp.bfloat16)
    rows_first, rows_second = neighbours[:RET], neighbours[RET:]

    lead = tail_rows // 8 * 8
    used = rows_here - lead
    valid = (jnp.arange(used) + lead >= tail_rows)[:, None]
    tokens = jnp.concatenate(
        [jnp.where(valid, hidden[lead:], 0), jnp.where(valid, grad_out[lead:], 0)], 0
    ).astype(jnp.bfloat16)
    token_cols = jnp.stack([move(tokens, to_chips(a, 0)) for a in range(n_half)])
    token_cols = jnp.concatenate(list(from_xor(token_cols, at_x)), 1)
    query_part = times(token_cols[:used], w_query)
    d_attn_part = contract(token_cols[used:], w_out)
    both = jnp.concatenate([query_part, d_attn_part], 0)
    both = (both + other_core(both)).astype(jnp.bfloat16)
    query, d_attn = both[:used], both[used:]

    head_of = jnp.arange(width)[None, :] // HD
    is_head = head_of == jnp.arange(heads_here)[:, None]
    key_dirs = contract(jnp.where(is_head, query[used - 1 :], 0), w_key)
    value_dirs = contract(jnp.where(is_head, d_attn[used - 1 :], 0), w_value)
    dirs = jnp.concatenate([value_dirs, key_dirs], 0).astype(jnp.bfloat16)
    dirs = dirs.reshape(2 * heads_here, n_half, cols_here)
    dirs = from_xor(jnp.transpose(dirs, (1, 0, 2)), at_x)
    pieces = [(a, b) for b in range(n_group) for a in range(n_half)]
    all_dirs = jnp.stack([move(dirs[a], to_columns(a, b)) for a, b in pieces])
    all_dirs = from_xor(all_dirs, at_g * n_half + at_x)
    all_dirs = all_dirs.reshape(n_mp, 2, heads_here, cols_here)
    all_dirs = jnp.transpose(all_dirs, (1, 0, 2, 3)).reshape(-1, cols_here)
    all_heads = n_mp * heads_here
    along = contract(all_dirs, rows_second)
    step = 1
    while step < n_mp:
        along = along + move(along, lambda d, m, g: (d, m ^ step, g))
        step *= 2
    live_second = (counts[1] > at_g).astype(jnp.float32)
    d_prob_second, score_second = along[:all_heads], along[all_heads:] * inv_root
    weight_second = jnp.exp(score_second) * live_second
    sums = jnp.stack([jnp.sum(weight_second, -1), jnp.sum(weight_second * d_prob_second, -1)])
    sums = sums + other_core(sums)
    total_second = 1.0 + sums[0]
    prob_second = weight_second / total_second[:, None]
    d_score_second = prob_second * (d_prob_second - (sums[1] / total_second)[:, None])
    mixed = jnp.concatenate([prob_second, d_score_second * inv_root], 0).astype(jnp.bfloat16)
    grad_second = lax.dot_general(
        mixed, all_dirs, (((0,), (0,)), ((), ())), preferred_element_type=jnp.float32
    )
    blends = times(mixed, rows_second).astype(jnp.bfloat16)
    blends = blends.reshape(2, n_mp, heads_here, cols_here)
    blends = from_xor(jnp.transpose(blends, (1, 0, 2, 3)), at_g * n_half + at_x)
    taken = [move(blends[i], to_chips(a, b)) for i, (a, b) in enumerate(pieces)]
    taken = jnp.stack(taken).reshape(n_group, n_half, 2 * heads_here, cols_here)
    taken = jnp.sum(taken.astype(jnp.float32), 0).astype(jnp.bfloat16)
    taken = jnp.concatenate(list(from_xor(taken, at_x)), 1)
    attn_second = jnp.sum(jnp.where(is_head, times(taken[:heads_here], w_value), 0), 0)
    d_query_second = jnp.sum(jnp.where(is_head, times(taken[heads_here:], w_key), 0), 0)
    second = jnp.stack([attn_second, d_query_second])
    second = (second + other_core(second)).astype(jnp.bfloat16)

    first = jnp.stack([move(rows_first, to_chips(a, b)) for a, b in pieces])
    first = first.reshape(n_group, n_half, RET, cols_here)
    first = from_xor(jnp.transpose(first, (1, 0, 2, 3)), at_x)
    first = jnp.concatenate(list(first.reshape(n_half, n_group * RET, cols_here)), 1)
    key_mine, key_other = halves(times(first, w_key))
    value_mine, value_other = halves(times(first, w_value))
    kv_other = other_core(jnp.concatenate([key_other, value_other], 0))
    n_keys = n_group * RET
    keys = (key_mine + kv_other[:n_keys]).astype(jnp.bfloat16)
    values = (value_mine + kv_other[n_keys:]).astype(jnp.bfloat16)
    in_first = (jnp.arange(used) < used - 1)[:, None]
    query_mine = jnp.where(in_first, halves(query)[0], 0)
    d_attn_mine = jnp.where(in_first, halves(d_attn)[0], 0)
    key_block = keys.reshape(n_keys, part_heads, HD)
    value_block = values.reshape(n_keys, part_heads, HD)
    query_block = query_mine.reshape(used, part_heads, HD)
    d_block = d_attn_mine.reshape(used, part_heads, HD)
    slot = jnp.repeat(jnp.arange(n_group), RET) ^ at_y
    live = (counts[0] > slot).astype(jnp.float32)
    scores = jnp.einsum("qhd,khd->hqk", query_block, key_block, preferred_element_type=jnp.float32)
    weights = jnp.exp(scores * inv_root) * live
    total = 1.0 + jnp.sum(weights, -1)
    numer = jnp.einsum(
        "hqk,khd->qhd", weights.astype(jnp.bfloat16), value_block, preferred_element_type=jnp.float32
    )
    attn = numer / jnp.transpose(total)[..., None]
    prob = weights / total[..., None]
    d_prob = jnp.einsum("qhd,khd->hqk", d_block, value_block, preferred_element_type=jnp.float32)
    delta = jnp.sum(d_block.astype(jnp.float32) * attn, -1)
    d_score = (prob * (d_prob - jnp.transpose(delta)[..., None])).astype(jnp.bfloat16)
    d_query = (
        jnp.einsum("hqk,khd->qhd", d_score, key_block, preferred_element_type=jnp.float32) * inv_root
    )
    d_keys = (
        jnp.einsum("hqk,qhd->khd", d_score, query_block, preferred_element_type=jnp.float32)
        * inv_root
    )
    d_values = jnp.einsum(
        "hqk,qhd->khd", prob.astype(jnp.bfloat16), d_block, preferred_element_type=jnp.float32
    )
    mine = jnp.concatenate([d_keys, d_values, attn, d_query], 0).astype(jnp.bfloat16)
    mine = mine.reshape(-1, part)
    other = other_core(mine)
    left, right = jnp.where(at_g == 0, mine, other), jnp.where(at_g == 0, other, mine)
    full = jnp.concatenate([left, right], 1)
    d_keys, d_values = full[:n_keys], full[n_keys : 2 * n_keys]
    attn, d_query = full[2 * n_keys : 2 * n_keys + used], full[2 * n_keys + used :]
    attn = jnp.where(in_first, attn, second[:1])
    d_query = jnp.where(in_first, d_query, second[1:])

    neigh = (contract(d_keys, w_key) + contract(d_values, w_value)).astype(jnp.bfloat16)
    neigh = neigh.reshape(n_group, RET, n_half, cols_here)
    neigh = from_xor(jnp.transpose(neigh, (2, 0, 1, 3)), at_x)
    grad_first = sum(
        move(neigh[a, b], to_columns(a, b)).astype(jnp.float32) for a, b in pieces
    )
    grad_neighbours = jnp.stack([grad_first, grad_second])[:, None]

    out_term = times(attn, w_out).astype(jnp.bfloat16).reshape(used, n_half, cols_here)
    hid_term = contract(d_query, w_query).astype(jnp.bfloat16).reshape(used, n_half, cols_here)
    terms = from_xor(jnp.stack([out_term, hid_term]), at_y)
    terms = from_xor(jnp.transpose(terms, (2, 0, 1, 3)), at_x)
    summed = sum(
        move(terms[a, b], to_columns(a, b)).astype(jnp.float32) for a, b in pieces
    )
    passed = other_core(summed)
    first_here = at_g == 0
    out_cols = jnp.where(valid, jnp.where(first_here, summed, passed), 0)
    hid_cols = jnp.where(valid, jnp.where(first_here, passed, summed), 0)
    zero_rows = jnp.zeros((lead, cols_here), jnp.float32)
    output = jnp.concatenate([zero_rows, out_cols], 0)
    grad_hidden = jnp.concatenate([zero_rows, hid_cols], 0)
    return (output, grad_hidden, grad_neighbours)


def solution(mesh):
    return jax.shard_map(
        per_device,
        mesh=mesh,
        in_specs=(
            P("dp", "mp"),
            P("dp", "group", None),
            P("dp"),
            P(("dp", "group"), "mp"),
            P("group", "mp"),
            P("group", "mp"),
            P("group", "mp"),
            P("mp", "group"),
            P("dp", "mp"),
        ),
        out_specs=(P("dp", "mp"), P("dp", "mp"), P("dp", "group", None, "mp")),
        check_vma=False,
    )
```

```python
import math

import jax
import jax.numpy as jnp
from jax import lax
from jax.experimental import pallas as pl
from jax.experimental.pallas import tpu as pltpu
from jax.sharding import PartitionSpec as P

HD = 128
BLOCK = 64
RET = 128
CAP = 64
AXES = ("dp", "mp", "group")


def contract(left, right):
    return lax.dot_general(
        left, right, (((1,), (1,)), ((), ())), preferred_element_type=jnp.float32
    )


def times(left, right):
    return jnp.dot(left, right, preferred_element_type=jnp.float32)


def from_xor(pieces, mask):
    count = pieces.shape[0]
    step = 1
    while step < count:
        split = pieces.reshape(count // (2 * step), 2, step, *pieces.shape[1:])
        swapped = jnp.concatenate([split[:, 1:], split[:, :1]], 1).reshape(pieces.shape)
        pieces = jnp.where((mask & step) != 0, swapped, pieces)
        step *= 2
    return pieces


def params(mib=20):
    return pltpu.CompilerParams(vmem_limit_bytes=mib * 1024 * 1024)


ANY = pl.BlockSpec(memory_space=pl.ANY)
HBM = pl.BlockSpec(memory_space=pltpu.HBM)
SMEM = pl.BlockSpec(memory_space=pltpu.SMEM)
VMEM = pl.BlockSpec(memory_space=pltpu.VMEM)
TILE = 512
COST = pl.CostEstimate(flops=0, bytes_accessed=0, transcendentals=0)


def call(kernel, out_shape, in_specs, name, scratch=(), mib=20):
    return pl.pallas_call(
        kernel,
        out_shape=out_shape,
        in_specs=in_specs,
        out_specs=jax.tree.map(lambda _: VMEM, out_shape),
        scratch_shapes=scratch,
        compiler_params=params(mib),
        cost_estimate=COST,
        name=name,
    )


def tiles(cols):
    tile = min(TILE, cols)
    return [slice(at, at + tile) for at in range(0, cols, tile)]


def load(sources, targets, sems):
    copies = [
        pltpu.make_async_copy(source, target, sems.at[i])
        for i, (source, target) in enumerate(zip(sources, targets))
    ]
    for copy in copies:
        copy.start()
    return lambda i: copies[i].wait()


def pick(weight, chip, there, cols, axis=0):
    size = there.stop - there.start
    rows = pl.ds(pl.multiple_of(chip * cols + there.start, size), size)
    return weight.at[rows] if axis == 0 else weight.at[:, rows]


def pair_scratch(width, depth, cols, extra=()):
    count = 2 * depth // min(TILE, cols)
    return (
        pltpu.VMEM((depth, width), jnp.bfloat16),
        pltpu.VMEM((depth, width), jnp.bfloat16),
        pltpu.SemaphoreType.DMA((count,)),
        *extra,
    )


def load_pair(chips, cols, first, second, first_room, second_room, sems):
    sources, targets, places = [], [], []
    for piece, chip in enumerate(chips):
        for there in tiles(cols):
            room = slice(piece * cols + there.start, piece * cols + there.stop)
            sources += [pick(first, chip, there, cols), pick(second, chip, there, cols)]
            targets += [first_room.at[room], second_room.at[room]]
            places.append((piece, there, room))
    return load(sources, targets, sems), places


def direction_kernel(chips, last, w_key, w_value, _, *refs):
    terms, (key_room, value_room, sems) = refs[:-3], refs[-3:]
    cols = terms[0].shape[1]
    where = [chips[piece] for piece in range(len(terms))]
    wait, places = load_pair(where, cols, w_key, w_value, key_room, value_room, sems)
    heads = terms[0].shape[0] // 2
    width = last.shape[1]
    head = lax.broadcasted_iota(jnp.int32, (heads, width), 0)
    own = head == lax.broadcasted_iota(jnp.int32, (heads, width), 1) // HD
    query = jnp.where(own, last[0:1], 0.0).astype(jnp.bfloat16)
    d_attn = jnp.where(own, last[1:2], 0.0).astype(jnp.bfloat16)
    for i, (piece, there, room) in enumerate(places):
        wait(2 * i)
        wait(2 * i + 1)
        both = [contract(d_attn, value_room[room]), contract(query, key_room[room])]
        terms[piece][:, there] = jnp.concatenate(both, 0).astype(jnp.bfloat16)


def directions(last, chips, w_key, w_value, cols, pieces, after):
    depth, width = w_key.shape
    return call(
        direction_kernel,
        (jax.ShapeDtypeStruct((2 * width // HD, cols), jnp.bfloat16),) * pieces,
        [SMEM, VMEM, HBM, HBM, ANY],
        "directions",
        pair_scratch(width, depth, cols),
        54,
    )(chips, last, w_key, w_value, after)


def settle_kernel(place, *refs):
    first, second = refs[-2:]
    for k in range(place.shape[0]):
        rows = jnp.concatenate([ref[k * CAP : (k + 1) * CAP] for ref in refs[:-3]], 0)
        rows = times(place[k], rows).astype(jnp.bfloat16)
        half = rows.shape[0] // 2
        first[k * half : (k + 1) * half] = rows[:half]
        second[k * half : (k + 1) * half] = rows[half:]


def settle(place, buffers, *after):
    heights = [place.shape[0] * place.shape[1] // 2] * 2
    cols = buffers[0].shape[1]
    tile = min(512, cols)
    return pl.pallas_call(
        settle_kernel,
        out_shape=tuple(jax.ShapeDtypeStruct((h, cols), jnp.bfloat16) for h in heights),
        grid=(cols // tile,),
        in_specs=[pl.BlockSpec(place.shape, lambda t: (0, 0, 0))]
        + [pl.BlockSpec((r.shape[0], tile), lambda t: (0, t)) for r in buffers]
        + [ANY] * len(after),
        out_specs=tuple(pl.BlockSpec((h, tile), lambda t: (0, t)) for h in heights),
        compiler_params=params(),
        cost_estimate=COST,
        name="settle",
    )(place, *buffers, *after)


def gather_terms_kernel(pieces, neighbours, place, *refs):
    mine, passed = refs[pieces:]
    rows = mine.shape[0]
    n_keys = neighbours * rows
    parts = [ref[...].astype(jnp.float32) for ref in refs[:pieces]]
    tokens = parts[-1] + sum(part[n_keys:] for part in parts[:-2])
    total = parts[-2] + sum(part[:n_keys] for part in parts[:-2])
    low, high = total[:rows], total[rows:]
    mine[...] = jnp.where(place[0] == 0, low, high)
    passed[:rows] = jnp.where(place[0] == 0, high, low).astype(jnp.bfloat16)
    passed[rows:] = tokens.astype(jnp.bfloat16)


def gather_terms(pieces, core, neighbours, rows):
    cols = pieces[0].shape[1]
    tile = min(TILE, cols)
    sent = rows + pieces[-1].shape[0]
    return pl.pallas_call(
        lambda *refs: gather_terms_kernel(len(pieces), neighbours, *refs),
        out_shape=(
            jax.ShapeDtypeStruct((rows, cols), jnp.float32),
            jax.ShapeDtypeStruct((sent, cols), jnp.bfloat16),
        ),
        grid=(cols // tile,),
        in_specs=[SMEM] + [pl.BlockSpec((p.shape[0], tile), lambda t: (0, t)) for p in pieces],
        out_specs=(
            pl.BlockSpec((rows, tile), lambda t: (0, t)),
            pl.BlockSpec((sent, tile), lambda t: (0, t)),
        ),
        compiler_params=params(),
        cost_estimate=COST,
        name="gather_terms",
    )(core[None], *pieces)


def finish_kernel(start, mine, passed, other, _, whole, out, hid):
    rows = mine.shape[0]
    whole[0] = mine[...] + other[:rows].astype(jnp.float32)
    both = passed[rows:].astype(jnp.float32) + other[rows:].astype(jnp.float32)
    used = both.shape[0] // 2
    lead = out.shape[0] - used
    valid = lax.broadcasted_iota(jnp.int32, (used, both.shape[1]), 0) + lead >= start
    for which, ref in enumerate((out, hid)):
        ref[:lead] = jnp.zeros((lead, both.shape[1]), jnp.float32)
        ref[lead:] = jnp.where(valid, both[which * used : (which + 1) * used], 0.0)


def finish(mine, passed, other, whole, tokens, start):
    rows, cols = mine.shape
    tile = min(TILE, cols)
    token_spec = pl.BlockSpec((tokens, tile), lambda t: (0, t))
    return pl.pallas_call(
        lambda *refs: finish_kernel(start, *refs),
        out_shape=(jax.ShapeDtypeStruct(whole.shape, whole.dtype),)
        + (jax.ShapeDtypeStruct((tokens, cols), jnp.float32),) * 2,
        grid=(cols // tile,),
        in_specs=[pl.BlockSpec((r.shape[0], tile), lambda t: (0, t)) for r in (mine, passed, other)]
        + [ANY],
        out_specs=(pl.BlockSpec((1, rows, tile), lambda t: (0, 0, t)), token_spec, token_spec),
        input_output_aliases={3: 0},
        compiler_params=params(),
        cost_estimate=COST,
        name="finish",
    )(mine, passed, other, whole)


def along_kernel(dirs, rows, along):
    along[...] = contract(dirs[...], rows[...])


def scores_along(dirs, rows):
    return call(
        along_kernel,
        jax.ShapeDtypeStruct((dirs.shape[0], rows.shape[0]), jnp.float32),
        [VMEM, VMEM],
        "scores_along",
    )(dirs, rows)


def blend_kernel(pieces, heads, place, *refs):
    rows, mixed = refs[pieces : pieces + 2]
    terms = refs[pieces + 2 :]
    along = sum(ref[...] for ref in refs[:pieces])
    all_heads = along.shape[0] // 2
    inv_root = 1.0 / math.sqrt(HD)
    d_prob, score = along[:all_heads], along[all_heads:] * inv_root
    live = lax.broadcasted_iota(jnp.int32, score.shape, 1) // RET < place[0]
    weight = jnp.exp(score) * live.astype(jnp.float32)
    prob = weight / (1.0 + jnp.sum(weight, 1, keepdims=True))
    d_score = prob * (d_prob - jnp.sum(prob * d_prob, 1, keepdims=True))
    both = jnp.concatenate([prob, d_score * inv_root], 0)
    mixed[...] = both
    both = both.astype(jnp.bfloat16)
    line = lax.broadcasted_iota(jnp.int32, (2 * heads, 2 * all_heads), 0)
    column = lax.broadcasted_iota(jnp.int32, (2 * heads, 2 * all_heads), 1)
    line = jnp.where(line < heads, line, line - heads + all_heads)
    for piece, term in enumerate(terms):
        chosen = (line + place[1 + piece] * heads == column).astype(jnp.bfloat16)
        part = times(chosen, both).astype(jnp.bfloat16)
        for there in tiles(rows.shape[1]):
            term[:, there] = times(part, rows[:, there]).astype(jnp.bfloat16)


def blend(along, rows, usable, chips, heads):
    cols = rows.shape[1]
    return call(
        lambda *refs: blend_kernel(len(along), heads, *refs),
        (jax.ShapeDtypeStruct(along[0].shape, jnp.float32),)
        + (jax.ShapeDtypeStruct((2 * heads, cols), jnp.bfloat16),) * chips.shape[0],
        [SMEM] + [VMEM] * (len(along) + 1),
        "blend",
    )(jnp.concatenate([usable[None], chips]), *along, rows)


def second_kernel(core, mixed, dirs, whole):
    rows = whole.shape[1]
    mine = mixed[:, pl.ds(pl.multiple_of(core[0] * rows, HD), rows)]
    whole[0] = times(jnp.transpose(mine).astype(jnp.bfloat16), dirs[...])


def second_grads(core, mixed, dirs):
    cols = dirs.shape[1]
    tile = min(TILE, cols)
    return pl.pallas_call(
        second_kernel,
        out_shape=jax.ShapeDtypeStruct((2, RET, cols), jnp.float32),
        grid=(cols // tile,),
        in_specs=[
            SMEM,
            pl.BlockSpec(mixed.shape, lambda t: (0, 0)),
            pl.BlockSpec((dirs.shape[0], tile), lambda t: (0, t)),
        ],
        out_specs=pl.BlockSpec((1, RET, tile), lambda t: (1, 0, t)),
        compiler_params=params(),
        cost_estimate=COST,
        name="second_grads",
    )(core[None], mixed, dirs)


def stage_kernel(count, *refs):
    wait = load(refs[:count], refs[count + 1 : -1], refs[-1])
    for i in range(count):
        wait(i)


def stage(weights, after):
    count = len(weights)
    return call(
        lambda *refs: stage_kernel(count, *refs),
        tuple(jax.ShapeDtypeStruct(w.shape, w.dtype) for w in weights),
        [HBM] * count + [ANY],
        "stage",
        (pltpu.SemaphoreType.DMA((count,)),),
    )(*weights, after)


def project_kernel(pieces, place, *refs):
    w_key, w_value, mine, other, blend_sums, sums = refs[2 * pieces :]
    n_keys, part = mine.shape[1:]
    first = True
    for piece in range(pieces):
        rows, blends = refs[2 * piece : 2 * piece + 2]
        cols = rows.shape[1]
        for there in tiles(cols):
            size = there.stop - there.start
            here = pl.ds(pl.multiple_of(place[1 + piece] * cols + there.start, size), size)
            both = jnp.concatenate([rows[:, there], blends[:, there]], 0)
            keys, values = times(both, w_key[here]), times(both, w_value[here])
            sums[0] = keys if first else sums[0] + keys
            sums[1] = values if first else sums[1] + values
            first = False
    core = place[0]
    mine[...] = sums[:, :n_keys, pl.ds(pl.multiple_of(core * part, HD), part)]
    other[...] = sums[:, :n_keys, pl.ds(pl.multiple_of((1 - core) * part, HD), part)]
    blend_sums[...] = sums[:, n_keys:]


def project(rows, blends, core, chips, w_key, w_value):
    n_keys, n_blends = rows[0].shape[0], blends[0].shape[0]
    width = w_key.shape[1]
    both = [part for pair in zip(rows, blends) for part in pair]
    half = jax.ShapeDtypeStruct((2, n_keys, width // 2), jnp.float32)
    return call(
        lambda *refs: project_kernel(len(rows), *refs),
        (half, half, jax.ShapeDtypeStruct((2, n_blends, width), jnp.float32)),
        [SMEM] + [VMEM] * (len(both) + 2),
        "project",
        (pltpu.VMEM((2, n_keys + n_blends, width), jnp.float32),),
    )(jnp.concatenate([core[None], chips]), *both, w_key, w_value)


def attend_kernel(place, mine, other, query, d_attn, *refs):
    core, usable = place[0], place[1]
    kv_grads, token_rows = refs[-2:]
    used = query.shape[0]
    n_keys, part = mine.shape[1:]
    inv_root = 1.0 / math.sqrt(HD)
    here = lax.broadcasted_iota(jnp.int32, (used, HD), 0) < used - 1
    key_row = lax.broadcasted_iota(jnp.int32, (n_keys, used), 0) // RET
    key_col = lax.broadcasted_iota(jnp.int32, (used, n_keys), 1) // RET
    live_row = (key_row < usable).astype(jnp.float32)
    live_col = (key_col < usable).astype(jnp.float32)
    for head in range(part // HD):
        cols = slice(head * HD, (head + 1) * HD)
        wide = pl.ds(pl.multiple_of(core * part + head * HD, HD), HD)
        keys = (mine[0, :, cols] + other[0, :, cols]).astype(jnp.bfloat16)
        values = (mine[1, :, cols] + other[1, :, cols]).astype(jnp.bfloat16)
        rows = jnp.where(here, query[:, wide].astype(jnp.float32), 0.0).astype(jnp.bfloat16)
        d_rows = jnp.where(here, d_attn[:, wide].astype(jnp.float32), 0.0)
        d_bf = d_rows.astype(jnp.bfloat16)
        weight = jnp.exp(contract(rows, keys) * inv_root) * live_col
        total = 1.0 + jnp.sum(weight, 1, keepdims=True)
        attn = times(weight.astype(jnp.bfloat16), values) / total
        delta = jnp.sum(d_rows * attn, 1, keepdims=True)
        d_score = (weight / total) * (contract(d_bf, values) - delta)
        d_query = times(d_score.astype(jnp.bfloat16), keys) * inv_root
        turned = jnp.exp(contract(keys, rows) * inv_root) * live_row
        prob = turned / (1.0 + jnp.sum(turned, 0, keepdims=True))
        d_prob = contract(values, d_bf)
        d_turned = prob * (d_prob - jnp.sum(prob * d_prob, 0, keepdims=True))
        d_keys = times(d_turned.astype(jnp.bfloat16), rows) * inv_root
        d_values = times(prob.astype(jnp.bfloat16), d_bf)
        kv_grads[0, :, cols] = d_keys.astype(jnp.bfloat16)
        kv_grads[1, :, cols] = d_values.astype(jnp.bfloat16)
        token_rows[0, :, cols] = attn.astype(jnp.bfloat16)
        token_rows[1, :, cols] = d_query.astype(jnp.bfloat16)


def attend(place, mine, other, query, d_attn):
    used = query.shape[0]
    n_keys, part = mine.shape[1:]
    return pl.pallas_call(
        attend_kernel,
        out_shape=(
            jax.ShapeDtypeStruct((2, n_keys, part), jnp.bfloat16),
            jax.ShapeDtypeStruct((2, used, part), jnp.bfloat16),
        ),
        in_specs=[pl.BlockSpec(memory_space=pltpu.SMEM)]
        + [VMEM] * 4,
        out_specs=(VMEM,) * 2,
        compiler_params=params(),
        cost_estimate=COST,
        name="attend",
    )(place, mine, other, query, d_attn)


def set_halves(core, mine, other, whole):
    part = mine.shape[-1]
    whole[:, :, pl.ds(pl.multiple_of(core * part, HD), part)] = mine[...]
    whole[:, :, pl.ds(pl.multiple_of((1 - core) * part, HD), part)] = other[...]


def term_kernel(place, *refs):
    kv, kv_other, tokens, tokens_other, last, w_key, w_value, w_out, w_query = refs[:9]
    whole, rows, key_room, value_room, sems, out_room, query_room, token_sems = refs[-8:]
    n_keys = kv.shape[1]
    used, width = rows.shape[1:]
    terms, token_terms = refs[10], refs[-9]
    cols = terms.shape[1]
    out_at = token_terms.shape[0] - 2 * used
    hid_at = out_at + used
    chip, core = place[0], place[1]
    wait, places = load_pair([chip], cols, w_key, w_value, key_room, value_room, sems)
    all_cols = slice(0, cols)
    wait_token = load(
        [pick(w_out, chip, all_cols, cols, 1), pick(w_query, chip, all_cols, cols)],
        [out_room, query_room],
        token_sems,
    )
    set_halves(core, kv, kv_other, whole)
    set_halves(core, tokens, tokens_other, rows)
    in_first = lax.broadcasted_iota(jnp.int32, (used, width), 0) < used - 1
    for which in range(2):
        merged = jnp.where(in_first, rows[which].astype(jnp.float32), last[which : which + 1])
        rows[which] = merged.astype(jnp.bfloat16)
    for i, (_, there, room) in enumerate(places):
        wait(2 * i)
        wait(2 * i + 1)
        term = contract(whole[0], key_room[room]) + contract(whole[1], value_room[room])
        terms[:n_keys, there] = term.astype(jnp.bfloat16)
    wait_token(0)
    wait_token(1)
    for there in tiles(cols):
        out_term = times(rows[0], out_room[:, there])
        token_terms[out_at:hid_at, there] = out_term.astype(jnp.bfloat16)
        hid_term = contract(rows[1], query_room[there])
        token_terms[hid_at:, there] = hid_term.astype(jnp.bfloat16)


def head_terms(place, kv, kv_other, tokens, tokens_other, last, weights, cols, after, split):
    n_keys, used, width = kv.shape[1], tokens.shape[1], weights[0].shape[1]
    heights = [n_keys, 2 * used] if split else [n_keys + 2 * used]
    extra = (
        pltpu.VMEM((width, cols), jnp.bfloat16),
        pltpu.VMEM((cols, width), jnp.bfloat16),
        pltpu.SemaphoreType.DMA((2,)),
    )
    return call(
        term_kernel,
        tuple(jax.ShapeDtypeStruct((height, cols), jnp.bfloat16) for height in heights),
        [SMEM] + [VMEM] * 5 + [HBM] * 4 + [ANY],
        "head_terms",
        (
            pltpu.VMEM((2, n_keys, width), jnp.bfloat16),
            pltpu.VMEM((2, used, width), jnp.bfloat16),
            *pair_scratch(width, cols, cols, extra),
        ),
        54,
    )(place, kv, kv_other, tokens, tokens_other, last, *weights, after)


def per_device(
    hidden, neighbour_ids, counts, embed_table, w_query, w_key, w_value, w_out, grad_out
):
    n_dp, n_mp, n_group = (lax.axis_size(name) for name in AXES)
    n_half = n_mp // n_group
    tail_rows = BLOCK - 1
    rows_here = hidden.shape[0]
    cols_here = hidden.shape[1]
    width = w_query.shape[1]
    heads_here = width // HD
    part = width // n_group
    inv_root = 1.0 / math.sqrt(HD)
    block_rows = embed_table.shape[0]
    at_d, at_m, at_g = (lax.axis_index(name) for name in AXES)
    at_y, at_x = at_m // n_half, at_m % n_half

    def move(array, target):
        pairs = []
        for d in range(n_dp):
            for m in range(n_mp):
                for g in range(n_group):
                    to_d, to_m, to_g = target(d, m, g)
                    here = (d * n_mp + m) * n_group + g
                    pairs.append((here, (to_d * n_mp + to_m) * n_group + to_g))
        return lax.ppermute(array, AXES, pairs)

    def to_owner(step_d, step_g):
        return lambda d, m, g: (d ^ step_d, m, g ^ step_g)

    def to_chips(a, b):
        return lambda d, m, g: (d, (g ^ b) * n_half + ((m % n_half) ^ a), m // n_half)

    def to_columns(a, b):
        return lambda d, m, g: (d, g * n_half + ((m % n_half) ^ a), (m // n_half) ^ b)

    def other_core(array):
        return move(array, lambda d, m, g: (d, m, g ^ 1))

    flat_ids = neighbour_ids.reshape(-1)
    slots = flat_ids.shape[0]
    other_ids = other_core(flat_ids)
    pair_ids = jnp.where(
        at_g == 0, jnp.stack([flat_ids, other_ids]), jnp.stack([other_ids, flat_ids])
    )
    every_id = [pair_ids]
    for step in range(1, n_dp):
        every_id.append(move(pair_ids, to_owner(step, 0)))
    every_id = jnp.stack(every_id)
    owner = at_d * n_group + at_g
    local_ids = every_id - owner * block_rows
    inside = (local_ids >= 0) & (local_ids < block_rows)
    before = jnp.triu(jnp.ones((slots, slots), jnp.bfloat16), 1)
    rank = times(inside.astype(jnp.bfloat16).reshape(-1, slots), before)
    rank = rank.reshape(inside.shape).astype(jnp.int32)
    slot_of = jnp.arange(CAP, dtype=jnp.int32)
    chosen = inside[:, :, None, :] & (rank[:, :, None, :] == slot_of[:, None])
    wanted = jnp.sum(jnp.where(chosen, local_ids[:, :, None, :], 0), -1)

    lead = tail_rows // 16 * 16
    used = rows_here - lead
    valid = (jnp.arange(used) + lead >= tail_rows)[:, None]
    hidden, grad_out, other_ids = lax.optimization_barrier((hidden, grad_out, other_ids))
    tokens = jnp.concatenate(
        [jnp.where(valid, hidden[lead:], 0), jnp.where(valid, grad_out[lead:], 0)], 0
    ).astype(jnp.bfloat16)
    token_cols = [move(tokens, to_chips(a, 0)) for a in range(n_half)]
    chips = at_x ^ jnp.arange(n_half, dtype=jnp.int32)
    token_cols = jnp.concatenate(list(from_xor(jnp.stack(token_cols), at_x)), 1)
    query_part = times(token_cols[:used], w_query)
    query_parts = jnp.concatenate([query_part, contract(token_cols[used:], w_out)], 0)
    looked_up = {}
    for step in reversed(range(n_dp)):
        rows = embed_table.at[wanted[step].reshape(-1)].get(mode="promise_in_bounds")
        wanted, looked_up[step] = lax.optimization_barrier((wanted, rows))
    received = {0: looked_up[0]}
    for step in reversed(range(1, n_dp)):
        if n_dp // 2 <= step < n_dp - 1:
            looked_up, received, query_parts = lax.optimization_barrier(
                (looked_up, received, query_parts)
            )
        received[step] = move(looked_up[step], to_owner(step, 0))
    received[0] = looked_up[0]
    buffers = []
    for step in range(n_dp):
        buffers += [received[step], other_core(received[step])]
    own_owner = pair_ids // block_rows
    same = own_owner[:, :, None] == own_owner[:, None, :]
    earlier = jnp.arange(slots)[None, :] < jnp.arange(slots)[:, None]
    own_rank = jnp.sum((same & earlier).astype(jnp.int32), -1)
    sender = jnp.stack(
        [(at_d ^ d) * n_group + (at_g ^ g) for d in range(n_dp) for g in range(n_group)]
    )
    place = (own_owner[:, :, None, None] == sender[:, None]) & (
        own_rank[:, :, None, None] == slot_of
    )
    place = place.astype(jnp.bfloat16).reshape(n_group, slots, -1)

    both = (query_parts + other_core(query_parts)).astype(jnp.bfloat16)
    query, d_attn = both[:used], both[used:]

    head_of = jnp.arange(width)[None, :] // HD
    is_head = head_of == jnp.arange(heads_here)[:, None]
    last = jnp.stack([query[used - 1], d_attn[used - 1]]).astype(jnp.float32)
    dirs = directions(last, chips, w_key, w_value, cols_here, n_half, received[0])
    pieces = [(a, b) for b in range(n_group) for a in range(n_half)]
    all_dirs = jnp.stack([move(dirs[a], to_columns(a, b)) for a, b in pieces])
    all_dirs = from_xor(all_dirs, at_g * n_half + at_x)
    all_dirs = all_dirs.reshape(n_mp, 2, heads_here, cols_here)
    all_dirs = jnp.transpose(all_dirs, (1, 0, 2, 3)).reshape(-1, cols_here)
    rows_first, rows_second = settle(place, buffers, all_dirs)
    first_cols = [move(rows_first, to_chips(a, 0)) for a in range(n_half)]
    along = scores_along(all_dirs, rows_second)
    along = [along] + [
        move(along, lambda d, m, g: (d, m ^ step, g)) for step in range(1, n_mp)
    ]
    mixed, *blends = blend(along, rows_second, counts[1], at_g * n_half + chips, heads_here)
    grads = second_grads(at_g, mixed, all_dirs)
    taken = [move(blends[a], to_chips(a, 0)) for a in range(n_half)]

    staged = stage([w_key, w_value], rows_second)
    kv_mine, kv_other, blend_sums = project(first_cols, taken, at_g, chips, *staged)
    d_query_second = jnp.sum(jnp.where(is_head, blend_sums[0, heads_here:], 0), 0)
    attn_second = jnp.sum(jnp.where(is_head, blend_sums[1, :heads_here], 0), 0)
    second = jnp.stack([attn_second, d_query_second])
    second = second + other_core(second)
    place = jnp.stack([at_g, counts[0]])
    kv_grads, token_rows = attend(place, kv_mine, other_core(kv_other), query, d_attn)
    token_other = other_core(token_rows)
    kv_other = other_core(kv_grads)

    sent = []
    after = second
    for a in reversed(range(n_half)):
        weights = (w_key, w_value, w_out, w_query)
        place = jnp.stack([at_x ^ a, at_g])
        rows = (kv_grads, kv_other, token_rows, token_other, second)
        terms = head_terms(place, *rows, weights, cols_here, after, a == 0)
        sent += [move(term, to_columns(a, 0)) for term in terms]
        after = terms[0]
    mine, passed = gather_terms(sent, at_g, n_group, RET)
    grads, output, grad_hidden = finish(
        mine, passed, other_core(passed), grads, rows_here, tail_rows
    )
    grad_neighbours = grads[:, None]
    return (output, grad_hidden, grad_neighbours)


def solution(mesh):
    return jax.shard_map(
        per_device,
        mesh=mesh,
        in_specs=(
            P("dp", "mp"),
            P("dp", "group", None),
            P("dp"),
            P(("dp", "group"), "mp"),
            P("group", "mp"),
            P("group", "mp"),
            P("group", "mp"),
            P("mp", "group"),
            P("dp", "mp"),
        ),
        out_specs=(P("dp", "mp"), P("dp", "mp"), P("dp", "group", None, "mp")),
        check_vma=False,
    )
```

```python
import math

import jax
import jax.numpy as jnp
from jax import lax
from jax.experimental import pallas as pl
from jax.experimental.pallas import tpu as pltpu
from jax.sharding import PartitionSpec as P

HD = 128
BLOCK = 64
RET = 128
CAP = 64
AXES = ("dp", "mp", "group")


def contract(left, right):
    return lax.dot_general(
        left, right, (((1,), (1,)), ((), ())), preferred_element_type=jnp.float32
    )


def times(left, right):
    return jnp.dot(left, right, preferred_element_type=jnp.float32)


def from_xor(pieces, mask):
    count = pieces.shape[0]
    step = 1
    while step < count:
        split = pieces.reshape(count // (2 * step), 2, step, *pieces.shape[1:])
        swapped = jnp.concatenate([split[:, 1:], split[:, :1]], 1).reshape(pieces.shape)
        pieces = jnp.where((mask & step) != 0, swapped, pieces)
        step *= 2
    return pieces


def params(mib=20):
    return pltpu.CompilerParams(vmem_limit_bytes=mib * 1024 * 1024)


ANY = pl.BlockSpec(memory_space=pl.ANY)
HBM = pl.BlockSpec(memory_space=pltpu.HBM)
SMEM = pl.BlockSpec(memory_space=pltpu.SMEM)
VMEM = pl.BlockSpec(memory_space=pltpu.VMEM)
TILE = 512
COST = pl.CostEstimate(flops=0, bytes_accessed=0, transcendentals=0)


def call(kernel, out_shape, in_specs, name, scratch=(), mib=20):
    return pl.pallas_call(
        kernel,
        out_shape=out_shape,
        in_specs=in_specs,
        out_specs=jax.tree.map(lambda _: VMEM, out_shape),
        scratch_shapes=scratch,
        compiler_params=params(mib),
        cost_estimate=COST,
        name=name,
    )


def tiles(cols):
    tile = min(TILE, cols)
    return [slice(at, at + tile) for at in range(0, cols, tile)]


def load(sources, targets, sems):
    copies = [
        pltpu.make_async_copy(source, target, sems.at[i])
        for i, (source, target) in enumerate(zip(sources, targets))
    ]
    for copy in copies:
        copy.start()
    return lambda i: copies[i].wait()


def pick(weight, chip, there, cols, axis=0):
    size = there.stop - there.start
    rows = pl.ds(pl.multiple_of(chip * cols + there.start, size), size)
    return weight.at[rows] if axis == 0 else weight.at[:, rows]


def pair_scratch(width, depth, cols, extra=()):
    count = 2 * depth // min(TILE, cols)
    return (
        pltpu.VMEM((depth, width), jnp.bfloat16),
        pltpu.VMEM((depth, width), jnp.bfloat16),
        pltpu.SemaphoreType.DMA((count,)),
        *extra,
    )


def load_pair(chips, cols, first, second, first_room, second_room, sems):
    sources, targets, places = [], [], []
    for piece, chip in enumerate(chips):
        for there in tiles(cols):
            room = slice(piece * cols + there.start, piece * cols + there.stop)
            sources += [pick(first, chip, there, cols), pick(second, chip, there, cols)]
            targets += [first_room.at[room], second_room.at[room]]
            places.append((piece, there, room))
    return load(sources, targets, sems), places


def query_kernel(pieces, chips, *refs):
    w_query, w_out, sums, query_room, out_room, query_sems, out_sems = refs[pieces:]
    used = sums.shape[0] // 2
    cols = refs[0].shape[1]
    places = [(piece, there) for piece in range(pieces) for there in tiles(cols)]
    rooms = [
        slice(piece * cols + there.start, piece * cols + there.stop) for piece, there in places
    ]
    wait_query = load(
        [pick(w_query, chips[piece], there, cols) for piece, there in places],
        [query_room.at[room] for room in rooms],
        query_sems,
    )
    wait_out = load(
        [pick(w_out, chips[piece], there, cols, 1) for piece, there in places],
        [out_room.at[:, room] for room in rooms],
        out_sems,
    )
    for i, ((piece, there), room) in enumerate(zip(places, rooms)):
        tokens = refs[piece]
        wait_query(i)
        query = times(tokens[:used, there], query_room[room])
        sums[:used] = query if i == 0 else sums[:used] + query
        wait_out(i)
        d_attn = contract(tokens[used:, there], out_room[:, room])
        sums[used:] = d_attn if i == 0 else sums[used:] + d_attn


def query_sums(tokens, chips, w_query, w_out):
    depth, width = w_query.shape
    count = depth // min(TILE, tokens[0].shape[1])
    return call(
        lambda *refs: query_kernel(len(tokens), *refs),
        jax.ShapeDtypeStruct((tokens[0].shape[0], width), jnp.float32),
        [SMEM] + [VMEM] * len(tokens) + [HBM, HBM],
        "query_sums",
        (
            pltpu.VMEM((depth, width), jnp.bfloat16),
            pltpu.VMEM((width, depth), jnp.bfloat16),
            pltpu.SemaphoreType.DMA((count,)),
            pltpu.SemaphoreType.DMA((count,)),
        ),
        50,
    )(chips, *tokens, w_query, w_out)


def direction_kernel(chips, last, w_key, w_value, _, *refs):
    terms, (key_room, value_room, sems) = refs[:-3], refs[-3:]
    cols = terms[0].shape[1]
    where = [chips[piece] for piece in range(len(terms))]
    wait, places = load_pair(where, cols, w_key, w_value, key_room, value_room, sems)
    heads = terms[0].shape[0] // 2
    width = last.shape[1]
    head = lax.broadcasted_iota(jnp.int32, (heads, width), 0)
    own = head == lax.broadcasted_iota(jnp.int32, (heads, width), 1) // HD
    query = jnp.where(own, last[0:1], 0.0).astype(jnp.bfloat16)
    d_attn = jnp.where(own, last[1:2], 0.0).astype(jnp.bfloat16)
    for i, (piece, there, room) in enumerate(places):
        wait(2 * i)
        wait(2 * i + 1)
        both = [contract(d_attn, value_room[room]), contract(query, key_room[room])]
        terms[piece][:, there] = jnp.concatenate(both, 0).astype(jnp.bfloat16)


def directions(last, chips, w_key, w_value, cols, pieces, after):
    depth, width = w_key.shape
    return call(
        direction_kernel,
        (jax.ShapeDtypeStruct((2 * width // HD, cols), jnp.bfloat16),) * pieces,
        [SMEM, VMEM, HBM, HBM, ANY],
        "directions",
        pair_scratch(width, depth, cols),
        54,
    )(chips, last, w_key, w_value, after)


def settle_kernel(place, *refs):
    first, second = refs[-2:]
    for k in range(place.shape[0]):
        rows = jnp.concatenate([ref[k * CAP : (k + 1) * CAP] for ref in refs[:-3]], 0)
        rows = times(place[k], rows).astype(jnp.bfloat16)
        half = rows.shape[0] // 2
        first[k * half : (k + 1) * half] = rows[:half]
        second[k * half : (k + 1) * half] = rows[half:]


def settle(place, buffers, *after):
    heights = [place.shape[0] * place.shape[1] // 2] * 2
    cols = buffers[0].shape[1]
    tile = min(512, cols)
    return pl.pallas_call(
        settle_kernel,
        out_shape=tuple(jax.ShapeDtypeStruct((h, cols), jnp.bfloat16) for h in heights),
        grid=(cols // tile,),
        in_specs=[pl.BlockSpec(place.shape, lambda t: (0, 0, 0))]
        + [pl.BlockSpec((r.shape[0], tile), lambda t: (0, t)) for r in buffers]
        + [ANY] * len(after),
        out_specs=tuple(pl.BlockSpec((h, tile), lambda t: (0, t)) for h in heights),
        compiler_params=params(),
        cost_estimate=COST,
        name="settle",
    )(place, *buffers, *after)


def gather_terms_kernel(pieces, neighbours, place, *refs):
    mine, passed = refs[pieces:]
    rows = mine.shape[0]
    parts = [ref[...].astype(jnp.float32) for ref in refs[:pieces]]
    total, tokens = sum(parts[: pieces // 2]), sum(parts[pieces // 2 :])
    low, high = total[:rows], total[rows:]
    mine[...] = jnp.where(place[0] == 0, low, high)
    passed[:rows] = jnp.where(place[0] == 0, high, low).astype(jnp.bfloat16)
    passed[rows:] = tokens.astype(jnp.bfloat16)


def gather_terms(pieces, core, neighbours, rows):
    cols = pieces[0].shape[1]
    tile = min(TILE, cols)
    sent = rows + pieces[-1].shape[0]
    return pl.pallas_call(
        lambda *refs: gather_terms_kernel(len(pieces), neighbours, *refs),
        out_shape=(
            jax.ShapeDtypeStruct((rows, cols), jnp.float32),
            jax.ShapeDtypeStruct((sent, cols), jnp.bfloat16),
        ),
        grid=(cols // tile,),
        in_specs=[SMEM] + [pl.BlockSpec((p.shape[0], tile), lambda t: (0, t)) for p in pieces],
        out_specs=(
            pl.BlockSpec((rows, tile), lambda t: (0, t)),
            pl.BlockSpec((sent, tile), lambda t: (0, t)),
        ),
        compiler_params=params(),
        cost_estimate=COST,
        name="gather_terms",
    )(core[None], *pieces)


def finish_kernel(start, mine, passed, other, _, whole, out, hid):
    rows = mine.shape[0]
    whole[0] = mine[...] + other[:rows].astype(jnp.float32)
    both = passed[rows:].astype(jnp.float32) + other[rows:].astype(jnp.float32)
    used = both.shape[0] // 2
    lead = out.shape[0] - used
    valid = lax.broadcasted_iota(jnp.int32, (used, both.shape[1]), 0) + lead >= start
    for which, ref in enumerate((out, hid)):
        ref[:lead] = jnp.zeros((lead, both.shape[1]), jnp.float32)
        ref[lead:] = jnp.where(valid, both[which * used : (which + 1) * used], 0.0)


def finish(mine, passed, other, whole, tokens, start):
    rows, cols = mine.shape
    tile = min(TILE, cols)
    token_spec = pl.BlockSpec((tokens, tile), lambda t: (0, t))
    return pl.pallas_call(
        lambda *refs: finish_kernel(start, *refs),
        out_shape=(jax.ShapeDtypeStruct(whole.shape, whole.dtype),)
        + (jax.ShapeDtypeStruct((tokens, cols), jnp.float32),) * 2,
        grid=(cols // tile,),
        in_specs=[pl.BlockSpec((r.shape[0], tile), lambda t: (0, t)) for r in (mine, passed, other)]
        + [ANY],
        out_specs=(pl.BlockSpec((1, rows, tile), lambda t: (0, 0, t)), token_spec, token_spec),
        input_output_aliases={3: 0},
        compiler_params=params(),
        cost_estimate=COST,
        name="finish",
    )(mine, passed, other, whole)


def along_kernel(dirs, rows, along):
    along[...] = contract(dirs[...], rows[...])


def scores_along(dirs, rows):
    return call(
        along_kernel,
        jax.ShapeDtypeStruct((dirs.shape[0], rows.shape[0]), jnp.float32),
        [VMEM, VMEM],
        "scores_along",
    )(dirs, rows)


def blend_kernel(pieces, heads, place, *refs):
    rows, mixed = refs[pieces : pieces + 2]
    terms = refs[pieces + 2 :]
    along = sum(ref[...] for ref in refs[:pieces])
    all_heads = along.shape[0] // 2
    inv_root = 1.0 / math.sqrt(HD)
    d_prob, score = along[:all_heads], along[all_heads:] * inv_root
    live = lax.broadcasted_iota(jnp.int32, score.shape, 1) // RET < place[0]
    weight = jnp.exp(score) * live.astype(jnp.float32)
    prob = weight / (1.0 + jnp.sum(weight, 1, keepdims=True))
    d_score = prob * (d_prob - jnp.sum(prob * d_prob, 1, keepdims=True))
    both = jnp.concatenate([prob, d_score * inv_root], 0)
    mixed[...] = both
    both = both.astype(jnp.bfloat16)
    line = lax.broadcasted_iota(jnp.int32, (2 * heads, 2 * all_heads), 0)
    column = lax.broadcasted_iota(jnp.int32, (2 * heads, 2 * all_heads), 1)
    line = jnp.where(line < heads, line, line - heads + all_heads)
    for piece, term in enumerate(terms):
        chosen = (line + place[1 + piece] * heads == column).astype(jnp.bfloat16)
        part = times(chosen, both).astype(jnp.bfloat16)
        for there in tiles(rows.shape[1]):
            term[:, there] = times(part, rows[:, there]).astype(jnp.bfloat16)


def blend(along, rows, usable, chips, heads):
    cols = rows.shape[1]
    return call(
        lambda *refs: blend_kernel(len(along), heads, *refs),
        (jax.ShapeDtypeStruct(along[0].shape, jnp.float32),)
        + (jax.ShapeDtypeStruct((2 * heads, cols), jnp.bfloat16),) * chips.shape[0],
        [SMEM] + [VMEM] * (len(along) + 1),
        "blend",
    )(jnp.concatenate([usable[None], chips]), *along, rows)


def second_kernel(core, mixed, dirs, whole):
    rows = whole.shape[1]
    mine = mixed[:, pl.ds(pl.multiple_of(core[0] * rows, HD), rows)]
    whole[0] = times(jnp.transpose(mine).astype(jnp.bfloat16), dirs[...])


def second_grads(core, mixed, dirs):
    cols = dirs.shape[1]
    tile = min(TILE, cols)
    return pl.pallas_call(
        second_kernel,
        out_shape=jax.ShapeDtypeStruct((2, RET, cols), jnp.float32),
        grid=(cols // tile,),
        in_specs=[
            SMEM,
            pl.BlockSpec(mixed.shape, lambda t: (0, 0)),
            pl.BlockSpec((dirs.shape[0], tile), lambda t: (0, t)),
        ],
        out_specs=pl.BlockSpec((1, RET, tile), lambda t: (1, 0, t)),
        compiler_params=params(),
        cost_estimate=COST,
        name="second_grads",
    )(core[None], mixed, dirs)


def stage_kernel(count, *refs):
    wait = load(refs[:count], refs[count + 1 : -1], refs[-1])
    for i in range(count):
        wait(i)


def stage(weights, after):
    count = len(weights)
    return call(
        lambda *refs: stage_kernel(count, *refs),
        tuple(jax.ShapeDtypeStruct(w.shape, w.dtype) for w in weights),
        [HBM] * count + [ANY],
        "stage",
        (pltpu.SemaphoreType.DMA((count,)),),
    )(*weights, after)


def project_kernel(pieces, place, *refs):
    w_key, w_value, mine, other, blend_sums, sums = refs[2 * pieces :]
    n_keys, part = mine.shape[1:]
    first = True
    for piece in range(pieces):
        rows, blends = refs[2 * piece : 2 * piece + 2]
        cols = rows.shape[1]
        for there in tiles(cols):
            size = there.stop - there.start
            here = pl.ds(pl.multiple_of(place[1 + piece] * cols + there.start, size), size)
            both = jnp.concatenate([rows[:, there], blends[:, there]], 0)
            keys, values = times(both, w_key[here]), times(both, w_value[here])
            sums[0] = keys if first else sums[0] + keys
            sums[1] = values if first else sums[1] + values
            first = False
    core = place[0]
    mine[...] = sums[:, :n_keys, pl.ds(pl.multiple_of(core * part, HD), part)]
    other[...] = sums[:, :n_keys, pl.ds(pl.multiple_of((1 - core) * part, HD), part)]
    blend_sums[...] = sums[:, n_keys:]


def project(rows, blends, core, chips, w_key, w_value):
    n_keys, n_blends = rows[0].shape[0], blends[0].shape[0]
    width = w_key.shape[1]
    both = [part for pair in zip(rows, blends) for part in pair]
    half = jax.ShapeDtypeStruct((2, n_keys, width // 2), jnp.float32)
    return call(
        lambda *refs: project_kernel(len(rows), *refs),
        (half, half, jax.ShapeDtypeStruct((2, n_blends, width), jnp.float32)),
        [SMEM] + [VMEM] * (len(both) + 2),
        "project",
        (pltpu.VMEM((2, n_keys + n_blends, width), jnp.float32),),
    )(jnp.concatenate([core[None], chips]), *both, w_key, w_value)


def attend_kernel(place, mine, other, query, d_attn, *refs):
    core, usable = place[0], place[1]
    kv_grads, token_rows = refs[-2:]
    used = query.shape[0]
    n_keys, part = mine.shape[1:]
    inv_root = 1.0 / math.sqrt(HD)
    here = lax.broadcasted_iota(jnp.int32, (used, HD), 0) < used - 1
    key_row = lax.broadcasted_iota(jnp.int32, (n_keys, used), 0) // RET
    key_col = lax.broadcasted_iota(jnp.int32, (used, n_keys), 1) // RET
    live_row = (key_row < usable).astype(jnp.float32)
    live_col = (key_col < usable).astype(jnp.float32)
    for head in range(part // HD):
        cols = slice(head * HD, (head + 1) * HD)
        wide = pl.ds(pl.multiple_of(core * part + head * HD, HD), HD)
        keys = (mine[0, :, cols] + other[0, :, cols]).astype(jnp.bfloat16)
        values = (mine[1, :, cols] + other[1, :, cols]).astype(jnp.bfloat16)
        rows = jnp.where(here, query[:, wide].astype(jnp.float32), 0.0).astype(jnp.bfloat16)
        d_rows = jnp.where(here, d_attn[:, wide].astype(jnp.float32), 0.0)
        d_bf = d_rows.astype(jnp.bfloat16)
        weight = jnp.exp(contract(rows, keys) * inv_root) * live_col
        total = 1.0 + jnp.sum(weight, 1, keepdims=True)
        attn = times(weight.astype(jnp.bfloat16), values) / total
        delta = jnp.sum(d_rows * attn, 1, keepdims=True)
        d_score = (weight / total) * (contract(d_bf, values) - delta)
        d_query = times(d_score.astype(jnp.bfloat16), keys) * inv_root
        turned = jnp.exp(contract(keys, rows) * inv_root) * live_row
        prob = turned / (1.0 + jnp.sum(turned, 0, keepdims=True))
        d_prob = contract(values, d_bf)
        d_turned = prob * (d_prob - jnp.sum(prob * d_prob, 0, keepdims=True))
        d_keys = times(d_turned.astype(jnp.bfloat16), rows) * inv_root
        d_values = times(prob.astype(jnp.bfloat16), d_bf)
        kv_grads[0, :, cols] = d_keys.astype(jnp.bfloat16)
        kv_grads[1, :, cols] = d_values.astype(jnp.bfloat16)
        token_rows[0, :, cols] = attn.astype(jnp.bfloat16)
        token_rows[1, :, cols] = d_query.astype(jnp.bfloat16)


def attend(place, mine, other, query, d_attn):
    used = query.shape[0]
    n_keys, part = mine.shape[1:]
    return pl.pallas_call(
        attend_kernel,
        out_shape=(
            jax.ShapeDtypeStruct((2, n_keys, part), jnp.bfloat16),
            jax.ShapeDtypeStruct((2, used, part), jnp.bfloat16),
        ),
        in_specs=[pl.BlockSpec(memory_space=pltpu.SMEM)]
        + [VMEM] * 4,
        out_specs=(VMEM,) * 2,
        compiler_params=params(),
        cost_estimate=COST,
        name="attend",
    )(place, mine, other, query, d_attn)


def set_halves(core, mine, other, whole):
    part = mine.shape[-1]
    whole[:, :, pl.ds(pl.multiple_of(core * part, HD), part)] = mine[...]
    whole[:, :, pl.ds(pl.multiple_of((1 - core) * part, HD), part)] = other[...]


def neighbour_kernel(place, *refs):
    mine, other, w_key, w_value = refs[:4]
    terms, (whole, key_room, value_room, sems) = refs[4:-4], refs[-4:]
    cols = terms[0].shape[1]
    where = [place[1 + piece] for piece in range(len(terms))]
    wait, places = load_pair(where, cols, w_key, w_value, key_room, value_room, sems)
    set_halves(place[0], mine, other, whole)
    for i, (piece, there, room) in enumerate(places):
        wait(2 * i)
        wait(2 * i + 1)
        term = contract(whole[0], key_room[room]) + contract(whole[1], value_room[room])
        terms[piece][:, there] = term.astype(jnp.bfloat16)


def neighbour_terms(core, chips, mine, other, w_key, w_value, cols):
    n_keys = mine.shape[1]
    depth, width = w_key.shape
    return call(
        neighbour_kernel,
        (jax.ShapeDtypeStruct((n_keys, cols), jnp.bfloat16),) * chips.shape[0],
        [SMEM, VMEM, VMEM, HBM, HBM],
        "neighbour_terms",
        (pltpu.VMEM((2, n_keys, width), jnp.bfloat16), *pair_scratch(width, depth, cols)),
        54,
    )(jnp.concatenate([core[None], chips]), mine, other, w_key, w_value)


def token_kernel(place, *refs):
    mine, other, last, w_out, w_query = refs[:5]
    terms, (rows, out_room, query_room, sems) = refs[6:-4], refs[-4:]
    used, width = rows.shape[1:]
    cols = terms[0].shape[1]
    sources, targets = [], []
    for piece in range(len(terms)):
        chip, all_cols = place[1 + piece], slice(0, cols)
        sources += [pick(w_out, chip, all_cols, cols, 1), pick(w_query, chip, all_cols, cols)]
        room = slice(piece * cols, (piece + 1) * cols)
        targets += [out_room.at[:, room], query_room.at[room]]
    wait = load(sources, targets, sems)
    set_halves(place[0], mine, other, rows)
    in_first = lax.broadcasted_iota(jnp.int32, (used, width), 0) < used - 1
    for which in range(2):
        merged = jnp.where(in_first, rows[which].astype(jnp.float32), last[which : which + 1])
        rows[which] = merged.astype(jnp.bfloat16)
    for piece, term in enumerate(terms):
        wait(2 * piece)
        wait(2 * piece + 1)
        for there in tiles(cols):
            room = slice(piece * cols + there.start, piece * cols + there.stop)
            term[:used, there] = times(rows[0], out_room[:, room]).astype(jnp.bfloat16)
            term[used:, there] = contract(rows[1], query_room[room]).astype(jnp.bfloat16)


def token_terms(core, chips, mine, other, last, w_out, w_query, cols, after):
    used = mine.shape[1]
    depth, width = w_query.shape
    pieces = chips.shape[0]
    return call(
        token_kernel,
        (jax.ShapeDtypeStruct((2 * used, cols), jnp.bfloat16),) * pieces,
        [SMEM, VMEM, VMEM, VMEM, HBM, HBM, ANY],
        "token_terms",
        (
            pltpu.VMEM((2, used, width), jnp.bfloat16),
            pltpu.VMEM((width, depth), jnp.bfloat16),
            pltpu.VMEM((depth, width), jnp.bfloat16),
            pltpu.SemaphoreType.DMA((2 * pieces,)),
        ),
        54,
    )(jnp.concatenate([core[None], chips]), mine, other, last, w_out, w_query, after)


def per_device(
    hidden, neighbour_ids, counts, embed_table, w_query, w_key, w_value, w_out, grad_out
):
    n_dp, n_mp, n_group = (lax.axis_size(name) for name in AXES)
    n_half = n_mp // n_group
    tail_rows = BLOCK - 1
    rows_here = hidden.shape[0]
    cols_here = hidden.shape[1]
    width = w_query.shape[1]
    heads_here = width // HD
    part = width // n_group
    inv_root = 1.0 / math.sqrt(HD)
    block_rows = embed_table.shape[0]
    at_d, at_m, at_g = (lax.axis_index(name) for name in AXES)
    at_y, at_x = at_m // n_half, at_m % n_half

    def move(array, target):
        pairs = []
        for d in range(n_dp):
            for m in range(n_mp):
                for g in range(n_group):
                    to_d, to_m, to_g = target(d, m, g)
                    here = (d * n_mp + m) * n_group + g
                    pairs.append((here, (to_d * n_mp + to_m) * n_group + to_g))
        return lax.ppermute(array, AXES, pairs)

    def to_owner(step_d, step_g):
        return lambda d, m, g: (d ^ step_d, m, g ^ step_g)

    def to_chips(a, b):
        return lambda d, m, g: (d, (g ^ b) * n_half + ((m % n_half) ^ a), m // n_half)

    def to_columns(a, b):
        return lambda d, m, g: (d, g * n_half + ((m % n_half) ^ a), (m // n_half) ^ b)

    def other_core(array):
        return move(array, lambda d, m, g: (d, m, g ^ 1))

    flat_ids = neighbour_ids.reshape(-1)
    slots = flat_ids.shape[0]
    other_ids = other_core(flat_ids)
    pair_ids = jnp.where(
        at_g == 0, jnp.stack([flat_ids, other_ids]), jnp.stack([other_ids, flat_ids])
    )
    every_id = [pair_ids]
    for step in range(1, n_dp):
        every_id.append(move(pair_ids, to_owner(step, 0)))
    every_id = jnp.stack(every_id)
    owner = at_d * n_group + at_g
    local_ids = every_id - owner * block_rows
    inside = (local_ids >= 0) & (local_ids < block_rows)
    before = jnp.triu(jnp.ones((slots, slots), jnp.bfloat16), 1)
    rank = times(inside.astype(jnp.bfloat16).reshape(-1, slots), before)
    rank = rank.reshape(inside.shape).astype(jnp.int32)
    slot_of = jnp.arange(CAP, dtype=jnp.int32)
    chosen = inside[:, :, None, :] & (rank[:, :, None, :] == slot_of[:, None])
    wanted = jnp.sum(jnp.where(chosen, local_ids[:, :, None, :], 0), -1)

    lead = tail_rows // 16 * 16
    used = rows_here - lead
    valid = (jnp.arange(used) + lead >= tail_rows)[:, None]
    hidden, grad_out, other_ids = lax.optimization_barrier((hidden, grad_out, other_ids))
    tokens = jnp.concatenate(
        [jnp.where(valid, hidden[lead:], 0), jnp.where(valid, grad_out[lead:], 0)], 0
    ).astype(jnp.bfloat16)
    token_cols = [move(tokens, to_chips(a, 0)) for a in range(n_half)]
    chips = at_x ^ jnp.arange(n_half, dtype=jnp.int32)
    query_parts = query_sums(token_cols, chips, w_query, w_out)
    def look_up(step):
        return embed_table.at[wanted[step].reshape(-1)].get(mode="promise_in_bounds")

    looked_up = {}
    for step in reversed(range(1, n_dp)):
        wanted, looked_up[step] = lax.optimization_barrier((wanted, look_up(step)))
    received = {}
    for step in reversed(range(1, n_dp)):
        if n_dp // 2 <= step < n_dp - 1:
            looked_up, received, query_parts, wanted = lax.optimization_barrier(
                (looked_up, received, query_parts, wanted)
            )
        received[step] = move(looked_up[step], to_owner(step, 0))
    received[0] = look_up(0)
    buffers = []
    for step in range(n_dp):
        buffers += [received[step], other_core(received[step])]
    own_owner = pair_ids // block_rows
    same = own_owner[:, :, None] == own_owner[:, None, :]
    earlier = jnp.arange(slots)[None, :] < jnp.arange(slots)[:, None]
    own_rank = jnp.sum((same & earlier).astype(jnp.int32), -1)
    sender = jnp.stack(
        [(at_d ^ d) * n_group + (at_g ^ g) for d in range(n_dp) for g in range(n_group)]
    )
    place = (own_owner[:, :, None, None] == sender[:, None]) & (
        own_rank[:, :, None, None] == slot_of
    )
    place = place.astype(jnp.bfloat16).reshape(n_group, slots, -1)

    both = (query_parts + other_core(query_parts)).astype(jnp.bfloat16)
    query, d_attn = both[:used], both[used:]

    head_of = jnp.arange(width)[None, :] // HD
    is_head = head_of == jnp.arange(heads_here)[:, None]
    last = jnp.stack([query[used - 1], d_attn[used - 1]]).astype(jnp.float32)
    dirs = directions(last, chips, w_key, w_value, cols_here, n_half, received[0])
    pieces = [(a, b) for b in range(n_group) for a in range(n_half)]
    all_dirs = jnp.stack([move(dirs[a], to_columns(a, b)) for a, b in pieces])
    all_dirs = from_xor(all_dirs, at_g * n_half + at_x)
    all_dirs = all_dirs.reshape(n_mp, 2, heads_here, cols_here)
    all_dirs = jnp.transpose(all_dirs, (1, 0, 2, 3)).reshape(-1, cols_here)
    rows_first, rows_second = settle(place, buffers, all_dirs)
    along = scores_along(all_dirs, rows_second)
    along = [along] + [
        move(along, lambda d, m, g: (d, m ^ step, g)) for step in range(1, n_mp)
    ]
    rows_first, along = lax.optimization_barrier((rows_first, along))
    first_cols = [move(rows_first, to_chips(a, 0)) for a in range(n_half)]
    mixed, *blends = blend(along, rows_second, counts[1], at_g * n_half + chips, heads_here)
    grads = second_grads(at_g, mixed, all_dirs)
    taken = [move(blends[a], to_chips(a, 0)) for a in range(n_half)]

    staged = stage([w_key, w_value], rows_second)
    kv_mine, kv_other, blend_sums = project(first_cols, taken, at_g, chips, *staged)
    d_query_second = jnp.sum(jnp.where(is_head, blend_sums[0, heads_here:], 0), 0)
    attn_second = jnp.sum(jnp.where(is_head, blend_sums[1, :heads_here], 0), 0)
    second = jnp.stack([attn_second, d_query_second])
    second = second + other_core(second)
    place = jnp.stack([at_g, counts[0]])
    kv_grads, token_rows = attend(place, kv_mine, other_core(kv_other), query, d_attn)
    token_other = other_core(token_rows)
    kv_other = other_core(kv_grads)

    neigh = neighbour_terms(at_g, chips, kv_grads, kv_other, w_key, w_value, cols_here)
    terms = token_terms(
        at_g, chips, token_rows, token_other, second, w_out, w_query, cols_here, neigh[0]
    )
    sent = [move(part[a], to_columns(a, 0)) for part in (neigh, terms) for a in range(n_half)]
    mine, passed = gather_terms(sent, at_g, n_group, RET)
    grads, output, grad_hidden = finish(
        mine, passed, other_core(passed), grads, rows_here, tail_rows
    )
    grad_neighbours = grads[:, None]
    return (output, grad_hidden, grad_neighbours)


def solution(mesh):
    return jax.shard_map(
        per_device,
        mesh=mesh,
        in_specs=(
            P("dp", "mp"),
            P("dp", "group", None),
            P("dp"),
            P(("dp", "group"), "mp"),
            P("group", "mp"),
            P("group", "mp"),
            P("group", "mp"),
            P("mp", "group"),
            P("dp", "mp"),
        ),
        out_specs=(P("dp", "mp"), P("dp", "mp"), P("dp", "group", None, "mp")),
        check_vma=False,
    )
```

```python
import math

import jax
import jax.numpy as jnp
from jax import lax
from jax.experimental import pallas as pl
from jax.experimental.pallas import tpu as pltpu
from jax.sharding import PartitionSpec as P

HD = 128
BLOCK = 64
RET = 128
CAP = 64
AXES = ("dp", "mp", "group")


def contract(left, right):
    return lax.dot_general(
        left, right, (((1,), (1,)), ((), ())), preferred_element_type=jnp.float32
    )


def times(left, right):
    return jnp.dot(left, right, preferred_element_type=jnp.float32)


def from_xor(pieces, mask):
    count = pieces.shape[0]
    step = 1
    while step < count:
        split = pieces.reshape(count // (2 * step), 2, step, *pieces.shape[1:])
        swapped = jnp.concatenate([split[:, 1:], split[:, :1]], 1).reshape(pieces.shape)
        pieces = jnp.where((mask & step) != 0, swapped, pieces)
        step *= 2
    return pieces


def params(mib=20):
    return pltpu.CompilerParams(vmem_limit_bytes=mib * 1024 * 1024)


ANY = pl.BlockSpec(memory_space=pl.ANY)
HBM = pl.BlockSpec(memory_space=pltpu.HBM)
SMEM = pl.BlockSpec(memory_space=pltpu.SMEM)
VMEM = pl.BlockSpec(memory_space=pltpu.VMEM)
TILE = 512
COST = pl.CostEstimate(flops=0, bytes_accessed=0, transcendentals=0)


def call(kernel, out_shape, in_specs, name, scratch=(), mib=20, out_spec=VMEM):
    return pl.pallas_call(
        kernel,
        out_shape=out_shape,
        in_specs=in_specs,
        out_specs=jax.tree.map(lambda _: out_spec, out_shape),
        scratch_shapes=scratch,
        compiler_params=params(mib),
        cost_estimate=COST,
        name=name,
    )


def tiles(cols):
    tile = min(TILE, cols)
    return [slice(at, at + tile) for at in range(0, cols, tile)]


def load(sources, targets, sems):
    copies = [
        pltpu.make_async_copy(source, target, sems.at[i])
        for i, (source, target) in enumerate(zip(sources, targets))
    ]
    for copy in copies:
        copy.start()
    return lambda i: copies[i].wait()


def pick(weight, chip, there, cols, axis=0):
    size = there.stop - there.start
    rows = pl.ds(pl.multiple_of(chip * cols + there.start, size), size)
    return weight.at[rows] if axis == 0 else weight.at[:, rows]


def pair_scratch(width, depth, cols, extra=()):
    count = 2 * depth // min(TILE, cols)
    return (
        pltpu.VMEM((depth, width), jnp.bfloat16),
        pltpu.VMEM((depth, width), jnp.bfloat16),
        pltpu.SemaphoreType.DMA((count,)),
        *extra,
    )


def load_pair(chips, cols, first, second, first_room, second_room, sems):
    sources, targets, places = [], [], []
    for piece, chip in enumerate(chips):
        for there in tiles(cols):
            room = slice(piece * cols + there.start, piece * cols + there.stop)
            sources += [pick(first, chip, there, cols), pick(second, chip, there, cols)]
            targets += [first_room.at[room], second_room.at[room]]
            places.append((piece, there, room))
    return load(sources, targets, sems), places


def query_kernel(pieces, chips, *refs):
    w_query, w_out, sums, query_room, out_room, query_sems, out_sems = refs[pieces:]
    used = sums.shape[0] // 2
    cols = refs[0].shape[1]
    places = [(piece, there) for piece in range(pieces) for there in tiles(cols)]
    rooms = [
        slice(piece * cols + there.start, piece * cols + there.stop) for piece, there in places
    ]
    wait_query = load(
        [pick(w_query, chips[piece], there, cols) for piece, there in places],
        [query_room.at[room] for room in rooms],
        query_sems,
    )
    wait_out = load(
        [pick(w_out, chips[piece], there, cols, 1) for piece, there in places],
        [out_room.at[:, room] for room in rooms],
        out_sems,
    )
    for i, ((piece, there), room) in enumerate(zip(places, rooms)):
        tokens = refs[piece]
        wait_query(i)
        query = times(tokens[:used, there], query_room[room])
        sums[:used] = query if i == 0 else sums[:used] + query
        wait_out(i)
        d_attn = contract(tokens[used:, there], out_room[:, room])
        sums[used:] = d_attn if i == 0 else sums[used:] + d_attn


def query_sums(tokens, chips, w_query, w_out):
    depth, width = w_query.shape
    count = depth // min(TILE, tokens[0].shape[1])
    return call(
        lambda *refs: query_kernel(len(tokens), *refs),
        jax.ShapeDtypeStruct((tokens[0].shape[0], width), jnp.float32),
        [SMEM] + [VMEM] * len(tokens) + [HBM, HBM],
        "query_sums",
        (
            pltpu.VMEM((depth, width), jnp.bfloat16),
            pltpu.VMEM((width, depth), jnp.bfloat16),
            pltpu.SemaphoreType.DMA((count,)),
            pltpu.SemaphoreType.DMA((count,)),
        ),
        50,
    )(chips, *tokens, w_query, w_out)


def direction_kernel(chips, last, w_key, w_value, _, *refs):
    terms, (key_room, value_room, sems) = refs[:-3], refs[-3:]
    cols = terms[0].shape[1]
    where = [chips[piece] for piece in range(len(terms))]
    wait, places = load_pair(where, cols, w_key, w_value, key_room, value_room, sems)
    heads = terms[0].shape[0] // 2
    width = last.shape[1]
    head = lax.broadcasted_iota(jnp.int32, (heads, width), 0)
    own = head == lax.broadcasted_iota(jnp.int32, (heads, width), 1) // HD
    query = jnp.where(own, last[0:1], 0.0).astype(jnp.bfloat16)
    d_attn = jnp.where(own, last[1:2], 0.0).astype(jnp.bfloat16)
    for i, (piece, there, room) in enumerate(places):
        wait(2 * i)
        wait(2 * i + 1)
        both = [contract(d_attn, value_room[room]), contract(query, key_room[room])]
        terms[piece][:, there] = jnp.concatenate(both, 0).astype(jnp.bfloat16)


def directions(last, chips, w_key, w_value, cols, pieces, after):
    depth, width = w_key.shape
    return call(
        direction_kernel,
        (jax.ShapeDtypeStruct((2 * width // HD, cols), jnp.bfloat16),) * pieces,
        [SMEM, VMEM, HBM, HBM, ANY],
        "directions",
        pair_scratch(width, depth, cols),
        54,
    )(chips, last, w_key, w_value, after)


def settle_kernel(place, *refs):
    first, second = refs[-2:]
    for k in range(place.shape[0]):
        rows = jnp.concatenate([ref[k * CAP : (k + 1) * CAP] for ref in refs[:-3]], 0)
        rows = times(place[k], rows).astype(jnp.bfloat16)
        half = rows.shape[0] // 2
        first[k * half : (k + 1) * half] = rows[:half]
        second[k * half : (k + 1) * half] = rows[half:]


def settle(place, buffers, *after):
    heights = [place.shape[0] * place.shape[1] // 2] * 2
    cols = buffers[0].shape[1]
    tile = min(512, cols)
    return pl.pallas_call(
        settle_kernel,
        out_shape=tuple(jax.ShapeDtypeStruct((h, cols), jnp.bfloat16) for h in heights),
        grid=(cols // tile,),
        in_specs=[pl.BlockSpec(place.shape, lambda t: (0, 0, 0))]
        + [pl.BlockSpec((r.shape[0], tile), lambda t: (0, t)) for r in buffers]
        + [ANY] * len(after),
        out_specs=tuple(pl.BlockSpec((h, tile), lambda t: (0, t)) for h in heights),
        compiler_params=params(),
        cost_estimate=COST,
        name="settle",
    )(place, *buffers, *after)


def gather_terms_kernel(pieces, neighbours, place, *refs):
    mine, passed = refs[pieces:]
    rows = mine.shape[0]
    parts = [ref[...].astype(jnp.float32) for ref in refs[:pieces]]
    total, tokens = sum(parts[: pieces // 2]), sum(parts[pieces // 2 :])
    low, high = total[:rows], total[rows:]
    mine[...] = jnp.where(place[0] == 0, low, high)
    passed[:rows] = jnp.where(place[0] == 0, high, low).astype(jnp.bfloat16)
    passed[rows:] = tokens.astype(jnp.bfloat16)


def gather_terms(pieces, core, neighbours, rows):
    cols = pieces[0].shape[1]
    tile = min(TILE, cols)
    sent = rows + pieces[-1].shape[0]
    return pl.pallas_call(
        lambda *refs: gather_terms_kernel(len(pieces), neighbours, *refs),
        out_shape=(
            jax.ShapeDtypeStruct((rows, cols), jnp.float32),
            jax.ShapeDtypeStruct((sent, cols), jnp.bfloat16),
        ),
        grid=(cols // tile,),
        in_specs=[SMEM] + [pl.BlockSpec((p.shape[0], tile), lambda t: (0, t)) for p in pieces],
        out_specs=(
            pl.BlockSpec((rows, tile), lambda t: (0, t)),
            pl.BlockSpec((sent, tile), lambda t: (0, t)),
        ),
        compiler_params=params(),
        cost_estimate=COST,
        name="gather_terms",
    )(core[None], *pieces)


def finish_kernel(start, mine, passed, other, _, whole, out, hid):
    rows = mine.shape[0]
    whole[0] = mine[...] + other[:rows].astype(jnp.float32)
    both = passed[rows:].astype(jnp.float32) + other[rows:].astype(jnp.float32)
    used = both.shape[0] // 2
    lead = out.shape[0] - used
    valid = lax.broadcasted_iota(jnp.int32, (used, both.shape[1]), 0) + lead >= start
    for which, ref in enumerate((out, hid)):
        ref[:lead] = jnp.zeros((lead, both.shape[1]), jnp.float32)
        ref[lead:] = jnp.where(valid, both[which * used : (which + 1) * used], 0.0)


def finish(mine, passed, other, whole, tokens, start):
    rows, cols = mine.shape
    tile = min(TILE, cols)
    token_spec = pl.BlockSpec((tokens, tile), lambda t: (0, t))
    return pl.pallas_call(
        lambda *refs: finish_kernel(start, *refs),
        out_shape=(jax.ShapeDtypeStruct(whole.shape, whole.dtype),)
        + (jax.ShapeDtypeStruct((tokens, cols), jnp.float32),) * 2,
        grid=(cols // tile,),
        in_specs=[pl.BlockSpec((r.shape[0], tile), lambda t: (0, t)) for r in (mine, passed, other)]
        + [ANY],
        out_specs=(pl.BlockSpec((1, rows, tile), lambda t: (0, 0, t)), token_spec, token_spec),
        input_output_aliases={3: 0},
        compiler_params=params(),
        cost_estimate=COST,
        name="finish",
    )(mine, passed, other, whole)


def along_kernel(dirs, rows, along):
    along[...] = contract(dirs[...], rows[...])


def scores_along(dirs, rows):
    return call(
        along_kernel,
        jax.ShapeDtypeStruct((dirs.shape[0], rows.shape[0]), jnp.float32),
        [VMEM, VMEM],
        "scores_along",
    )(dirs, rows)


def blend_kernel(pieces, heads, place, *refs):
    rows, mixed = refs[pieces : pieces + 2]
    terms = refs[pieces + 2 :]
    along = sum(ref[...] for ref in refs[:pieces])
    all_heads = along.shape[0] // 2
    inv_root = 1.0 / math.sqrt(HD)
    d_prob, score = along[:all_heads], along[all_heads:] * inv_root
    live = lax.broadcasted_iota(jnp.int32, score.shape, 1) // RET < place[0]
    weight = jnp.exp(score) * live.astype(jnp.float32)
    prob = weight / (1.0 + jnp.sum(weight, 1, keepdims=True))
    d_score = prob * (d_prob - jnp.sum(prob * d_prob, 1, keepdims=True))
    both = jnp.concatenate([prob, d_score * inv_root], 0)
    mixed[...] = both
    both = both.astype(jnp.bfloat16)
    line = lax.broadcasted_iota(jnp.int32, (2 * heads, 2 * all_heads), 0)
    column = lax.broadcasted_iota(jnp.int32, (2 * heads, 2 * all_heads), 1)
    line = jnp.where(line < heads, line, line - heads + all_heads)
    for piece, term in enumerate(terms):
        chosen = (line + place[1 + piece] * heads == column).astype(jnp.bfloat16)
        part = times(chosen, both).astype(jnp.bfloat16)
        for there in tiles(rows.shape[1]):
            term[:, there] = times(part, rows[:, there]).astype(jnp.bfloat16)


def blend(along, rows, usable, chips, heads):
    cols = rows.shape[1]
    return call(
        lambda *refs: blend_kernel(len(along), heads, *refs),
        (jax.ShapeDtypeStruct(along[0].shape, jnp.float32),)
        + (jax.ShapeDtypeStruct((2 * heads, cols), jnp.bfloat16),) * chips.shape[0],
        [SMEM] + [VMEM] * (len(along) + 1),
        "blend",
    )(jnp.concatenate([usable[None], chips]), *along, rows)


def second_kernel(core, mixed, dirs, whole):
    rows = whole.shape[1]
    mine = mixed[:, pl.ds(pl.multiple_of(core[0] * rows, HD), rows)]
    whole[0] = times(jnp.transpose(mine).astype(jnp.bfloat16), dirs[...])


def second_grads(core, mixed, dirs):
    cols = dirs.shape[1]
    tile = min(TILE, cols)
    return pl.pallas_call(
        second_kernel,
        out_shape=jax.ShapeDtypeStruct((2, RET, cols), jnp.float32),
        grid=(cols // tile,),
        in_specs=[
            SMEM,
            pl.BlockSpec(mixed.shape, lambda t: (0, 0)),
            pl.BlockSpec((dirs.shape[0], tile), lambda t: (0, t)),
        ],
        out_specs=pl.BlockSpec((1, RET, tile), lambda t: (1, 0, t)),
        compiler_params=params(),
        cost_estimate=COST,
        name="second_grads",
    )(core[None], mixed, dirs)


def stage_kernel(count, *refs):
    wait = load(refs[:count], refs[count + 1 : -1], refs[-1])
    for i in range(count):
        wait(i)


def stage(weights, after):
    count = len(weights)
    return call(
        lambda *refs: stage_kernel(count, *refs),
        tuple(jax.ShapeDtypeStruct(w.shape, w.dtype) for w in weights),
        [HBM] * count + [ANY],
        "stage",
        (pltpu.SemaphoreType.DMA((count,)),),
    )(*weights, after)


def project_kernel(pieces, place, *refs):
    w_key, w_value, mine, other, blend_sums, sums = refs[2 * pieces :]
    n_keys, part = mine.shape[1:]
    first = True
    for piece in range(pieces):
        rows, blends = refs[2 * piece : 2 * piece + 2]
        cols = rows.shape[1]
        for there in tiles(cols):
            size = there.stop - there.start
            here = pl.ds(pl.multiple_of(place[1 + piece] * cols + there.start, size), size)
            both = jnp.concatenate([rows[:, there], blends[:, there]], 0)
            keys, values = times(both, w_key[here]), times(both, w_value[here])
            sums[0] = keys if first else sums[0] + keys
            sums[1] = values if first else sums[1] + values
            first = False
    core = place[0]
    mine[...] = sums[:, :n_keys, pl.ds(pl.multiple_of(core * part, HD), part)]
    other[...] = sums[:, :n_keys, pl.ds(pl.multiple_of((1 - core) * part, HD), part)]
    blend_sums[...] = sums[:, n_keys:]


def project(rows, blends, core, chips, w_key, w_value):
    n_keys, n_blends = rows[0].shape[0], blends[0].shape[0]
    width = w_key.shape[1]
    both = [part for pair in zip(rows, blends) for part in pair]
    half = jax.ShapeDtypeStruct((2, n_keys, width // 2), jnp.float32)
    return call(
        lambda *refs: project_kernel(len(rows), *refs),
        (half, half, jax.ShapeDtypeStruct((2, n_blends, width), jnp.float32)),
        [SMEM] + [VMEM] * (len(both) + 2),
        "project",
        (pltpu.VMEM((2, n_keys + n_blends, width), jnp.float32),),
    )(jnp.concatenate([core[None], chips]), *both, w_key, w_value)


def attend_kernel(place, mine, other, query, d_attn, *refs):
    core, usable = place[0], place[1]
    kv_grads, token_rows = refs[-2:]
    used = query.shape[0]
    n_keys, part = mine.shape[1:]
    inv_root = 1.0 / math.sqrt(HD)
    here = lax.broadcasted_iota(jnp.int32, (used, HD), 0) < used - 1
    key_row = lax.broadcasted_iota(jnp.int32, (n_keys, used), 0) // RET
    key_col = lax.broadcasted_iota(jnp.int32, (used, n_keys), 1) // RET
    live_row = (key_row < usable).astype(jnp.float32)
    live_col = (key_col < usable).astype(jnp.float32)
    for head in range(part // HD):
        cols = slice(head * HD, (head + 1) * HD)
        wide = pl.ds(pl.multiple_of(core * part + head * HD, HD), HD)
        keys = (mine[0, :, cols] + other[0, :, cols]).astype(jnp.bfloat16)
        values = (mine[1, :, cols] + other[1, :, cols]).astype(jnp.bfloat16)
        rows = jnp.where(here, query[:, wide].astype(jnp.float32), 0.0).astype(jnp.bfloat16)
        d_rows = jnp.where(here, d_attn[:, wide].astype(jnp.float32), 0.0)
        d_bf = d_rows.astype(jnp.bfloat16)
        weight = jnp.exp(contract(rows, keys) * inv_root) * live_col
        total = 1.0 + jnp.sum(weight, 1, keepdims=True)
        attn = times(weight.astype(jnp.bfloat16), values) / total
        delta = jnp.sum(d_rows * attn, 1, keepdims=True)
        d_score = (weight / total) * (contract(d_bf, values) - delta)
        d_query = times(d_score.astype(jnp.bfloat16), keys) * inv_root
        turned = jnp.exp(contract(keys, rows) * inv_root) * live_row
        prob = turned / (1.0 + jnp.sum(turned, 0, keepdims=True))
        d_prob = contract(values, d_bf)
        d_turned = prob * (d_prob - jnp.sum(prob * d_prob, 0, keepdims=True))
        d_keys = times(d_turned.astype(jnp.bfloat16), rows) * inv_root
        d_values = times(prob.astype(jnp.bfloat16), d_bf)
        kv_grads[0, :, cols] = d_keys.astype(jnp.bfloat16)
        kv_grads[1, :, cols] = d_values.astype(jnp.bfloat16)
        token_rows[0, :, cols] = attn.astype(jnp.bfloat16)
        token_rows[1, :, cols] = d_query.astype(jnp.bfloat16)


def attend(place, mine, other, query, d_attn):
    used = query.shape[0]
    n_keys, part = mine.shape[1:]
    return pl.pallas_call(
        attend_kernel,
        out_shape=(
            jax.ShapeDtypeStruct((2, n_keys, part), jnp.bfloat16),
            jax.ShapeDtypeStruct((2, used, part), jnp.bfloat16),
        ),
        in_specs=[pl.BlockSpec(memory_space=pltpu.SMEM)]
        + [VMEM] * 4,
        out_specs=(VMEM,) * 2,
        compiler_params=params(),
        cost_estimate=COST,
        name="attend",
    )(place, mine, other, query, d_attn)


def set_halves(core, mine, other, whole):
    part = mine.shape[-1]
    whole[:, :, pl.ds(pl.multiple_of(core * part, HD), part)] = mine[...]
    whole[:, :, pl.ds(pl.multiple_of((1 - core) * part, HD), part)] = other[...]


def neighbour_kernel(place, *refs):
    mine, other, w_key, w_value = refs[:4]
    terms, rooms = refs[4:-6], refs[-6:]
    whole, key_room, value_room, sems, term_room, term_sems = rooms
    cols = terms[0].shape[1]
    where = [place[1 + piece] for piece in range(len(terms))]
    wait, places = load_pair(where, cols, w_key, w_value, key_room, value_room, sems)
    set_halves(place[0], mine, other, whole)
    copies = []
    for i, (piece, there, room) in enumerate(places):
        wait(2 * i)
        wait(2 * i + 1)
        term = contract(whole[0], key_room[room]) + contract(whole[1], value_room[room])
        term_room[:, room] = term.astype(jnp.bfloat16)
        target = terms[piece].at[:, there]
        copies.append(pltpu.make_async_copy(term_room.at[:, room], target, term_sems.at[i]))
        copies[-1].start()
    for copy in copies:
        copy.wait()


def neighbour_terms(core, chips, mine, other, w_key, w_value, cols):
    n_keys = mine.shape[1]
    depth, width = w_key.shape
    return call(
        neighbour_kernel,
        (jax.ShapeDtypeStruct((n_keys, cols), jnp.bfloat16),) * chips.shape[0],
        [SMEM, VMEM, VMEM, HBM, HBM],
        "neighbour_terms",
        (
            pltpu.VMEM((2, n_keys, width), jnp.bfloat16),
            *pair_scratch(width, depth, cols),
            pltpu.VMEM((n_keys, depth), jnp.bfloat16),
            pltpu.SemaphoreType.DMA((depth // min(TILE, cols),)),
        ),
        54,
        ANY,
    )(jnp.concatenate([core[None], chips]), mine, other, w_key, w_value)


def token_kernel(place, *refs):
    mine, other, last, w_out, w_query = refs[:5]
    terms, (rows, out_room, query_room, sems) = refs[6:-4], refs[-4:]
    used, width = rows.shape[1:]
    cols = terms[0].shape[1]
    sources, targets = [], []
    for piece in range(len(terms)):
        chip, all_cols = place[1 + piece], slice(0, cols)
        sources += [pick(w_out, chip, all_cols, cols, 1), pick(w_query, chip, all_cols, cols)]
        room = slice(piece * cols, (piece + 1) * cols)
        targets += [out_room.at[:, room], query_room.at[room]]
    wait = load(sources, targets, sems)
    set_halves(place[0], mine, other, rows)
    in_first = lax.broadcasted_iota(jnp.int32, (used, width), 0) < used - 1
    for which in range(2):
        merged = jnp.where(in_first, rows[which].astype(jnp.float32), last[which : which + 1])
        rows[which] = merged.astype(jnp.bfloat16)
    for piece, term in enumerate(terms):
        wait(2 * piece)
        wait(2 * piece + 1)
        for there in tiles(cols):
            room = slice(piece * cols + there.start, piece * cols + there.stop)
            term[:used, there] = times(rows[0], out_room[:, room]).astype(jnp.bfloat16)
            term[used:, there] = contract(rows[1], query_room[room]).astype(jnp.bfloat16)


def token_terms(core, chips, mine, other, last, w_out, w_query, cols, after):
    used = mine.shape[1]
    depth, width = w_query.shape
    pieces = chips.shape[0]
    return call(
        token_kernel,
        (jax.ShapeDtypeStruct((2 * used, cols), jnp.bfloat16),) * pieces,
        [SMEM, VMEM, VMEM, VMEM, HBM, HBM, ANY],
        "token_terms",
        (
            pltpu.VMEM((2, used, width), jnp.bfloat16),
            pltpu.VMEM((width, depth), jnp.bfloat16),
            pltpu.VMEM((depth, width), jnp.bfloat16),
            pltpu.SemaphoreType.DMA((2 * pieces,)),
        ),
        54,
    )(jnp.concatenate([core[None], chips]), mine, other, last, w_out, w_query, after)


def per_device(
    hidden, neighbour_ids, counts, embed_table, w_query, w_key, w_value, w_out, grad_out
):
    n_dp, n_mp, n_group = (lax.axis_size(name) for name in AXES)
    n_half = n_mp // n_group
    tail_rows = BLOCK - 1
    rows_here = hidden.shape[0]
    cols_here = hidden.shape[1]
    width = w_query.shape[1]
    heads_here = width // HD
    part = width // n_group
    inv_root = 1.0 / math.sqrt(HD)
    block_rows = embed_table.shape[0]
    at_d, at_m, at_g = (lax.axis_index(name) for name in AXES)
    at_y, at_x = at_m // n_half, at_m % n_half

    def move(array, target):
        pairs = []
        for d in range(n_dp):
            for m in range(n_mp):
                for g in range(n_group):
                    to_d, to_m, to_g = target(d, m, g)
                    here = (d * n_mp + m) * n_group + g
                    pairs.append((here, (to_d * n_mp + to_m) * n_group + to_g))
        return lax.ppermute(array, AXES, pairs)

    def to_owner(step_d, step_g):
        return lambda d, m, g: (d ^ step_d, m, g ^ step_g)

    def to_chips(a, b):
        return lambda d, m, g: (d, (g ^ b) * n_half + ((m % n_half) ^ a), m // n_half)

    def to_columns(a, b):
        return lambda d, m, g: (d, g * n_half + ((m % n_half) ^ a), (m // n_half) ^ b)

    def other_core(array):
        return move(array, lambda d, m, g: (d, m, g ^ 1))

    flat_ids = neighbour_ids.reshape(-1)
    slots = flat_ids.shape[0]
    other_ids = other_core(flat_ids)
    pair_ids = jnp.where(
        at_g == 0, jnp.stack([flat_ids, other_ids]), jnp.stack([other_ids, flat_ids])
    )
    every_id = [pair_ids]
    for step in range(1, n_dp):
        every_id.append(move(pair_ids, to_owner(step, 0)))
    every_id = jnp.stack(every_id)
    owner = at_d * n_group + at_g
    local_ids = every_id - owner * block_rows
    inside = (local_ids >= 0) & (local_ids < block_rows)
    before = jnp.triu(jnp.ones((slots, slots), jnp.bfloat16), 1)
    rank = times(inside.astype(jnp.bfloat16).reshape(-1, slots), before)
    rank = rank.reshape(inside.shape).astype(jnp.int32)
    slot_of = jnp.arange(CAP, dtype=jnp.int32)
    chosen = inside[:, :, None, :] & (rank[:, :, None, :] == slot_of[:, None])
    wanted = jnp.sum(jnp.where(chosen, local_ids[:, :, None, :], 0), -1)

    lead = tail_rows // 16 * 16
    used = rows_here - lead
    valid = (jnp.arange(used) + lead >= tail_rows)[:, None]
    hidden, grad_out, other_ids = lax.optimization_barrier((hidden, grad_out, other_ids))
    tokens = jnp.concatenate(
        [jnp.where(valid, hidden[lead:], 0), jnp.where(valid, grad_out[lead:], 0)], 0
    ).astype(jnp.bfloat16)
    token_cols = [move(tokens, to_chips(a, 0)) for a in range(n_half)]
    chips = at_x ^ jnp.arange(n_half, dtype=jnp.int32)
    query_parts = query_sums(token_cols, chips, w_query, w_out)
    def look_up(step):
        return embed_table.at[wanted[step].reshape(-1)].get(mode="promise_in_bounds")

    looked_up = {}
    for step in reversed(range(1, n_dp)):
        wanted, looked_up[step] = lax.optimization_barrier((wanted, look_up(step)))
    received = {}
    for step in reversed(range(1, n_dp)):
        if n_dp // 2 <= step < n_dp - 1:
            looked_up, received, query_parts, wanted = lax.optimization_barrier(
                (looked_up, received, query_parts, wanted)
            )
        received[step] = move(looked_up[step], to_owner(step, 0))
    received[0] = look_up(0)
    buffers = []
    for step in range(n_dp):
        buffers += [received[step], other_core(received[step])]
    own_owner = pair_ids // block_rows
    same = own_owner[:, :, None] == own_owner[:, None, :]
    earlier = jnp.arange(slots)[None, :] < jnp.arange(slots)[:, None]
    own_rank = jnp.sum((same & earlier).astype(jnp.int32), -1)
    sender = jnp.stack(
        [(at_d ^ d) * n_group + (at_g ^ g) for d in range(n_dp) for g in range(n_group)]
    )
    place = (own_owner[:, :, None, None] == sender[:, None]) & (
        own_rank[:, :, None, None] == slot_of
    )
    place = place.astype(jnp.bfloat16).reshape(n_group, slots, -1)

    both = (query_parts + other_core(query_parts)).astype(jnp.bfloat16)
    query, d_attn = both[:used], both[used:]

    head_of = jnp.arange(width)[None, :] // HD
    is_head = head_of == jnp.arange(heads_here)[:, None]
    last = jnp.stack([query[used - 1], d_attn[used - 1]]).astype(jnp.float32)
    dirs = directions(last, chips, w_key, w_value, cols_here, n_half, received[0])
    pieces = [(a, b) for b in range(n_group) for a in range(n_half)]
    all_dirs = jnp.stack([move(dirs[a], to_columns(a, b)) for a, b in pieces])
    all_dirs = from_xor(all_dirs, at_g * n_half + at_x)
    all_dirs = all_dirs.reshape(n_mp, 2, heads_here, cols_here)
    all_dirs = jnp.transpose(all_dirs, (1, 0, 2, 3)).reshape(-1, cols_here)
    rows_first, rows_second = settle(place, buffers, all_dirs)
    along = scores_along(all_dirs, rows_second)
    along = [along] + [
        move(along, lambda d, m, g: (d, m ^ step, g)) for step in range(1, n_mp)
    ]
    rows_first, along = lax.optimization_barrier((rows_first, along))
    first_cols = [move(rows_first, to_chips(a, 0)) for a in range(n_half)]
    mixed, *blends = blend(along, rows_second, counts[1], at_g * n_half + chips, heads_here)
    grads = second_grads(at_g, mixed, all_dirs)
    taken = [move(blends[a], to_chips(a, 0)) for a in range(n_half)]

    staged = stage([w_key, w_value], rows_second)
    kv_mine, kv_other, blend_sums = project(first_cols, taken, at_g, chips, *staged)
    d_query_second = jnp.sum(jnp.where(is_head, blend_sums[0, heads_here:], 0), 0)
    attn_second = jnp.sum(jnp.where(is_head, blend_sums[1, :heads_here], 0), 0)
    second = jnp.stack([attn_second, d_query_second])
    second = second + other_core(second)
    place = jnp.stack([at_g, counts[0]])
    kv_grads, token_rows = attend(place, kv_mine, other_core(kv_other), query, d_attn)
    token_other = other_core(token_rows)
    kv_other = other_core(kv_grads)

    neigh = neighbour_terms(at_g, chips, kv_grads, kv_other, w_key, w_value, cols_here)
    terms = token_terms(
        at_g, chips, token_rows, token_other, second, w_out, w_query, cols_here, neigh[0]
    )
    sent = [move(part[a], to_columns(a, 0)) for part in (neigh, terms) for a in range(n_half)]
    mine, passed = gather_terms(sent, at_g, n_group, RET)
    grads, output, grad_hidden = finish(
        mine, passed, other_core(passed), grads, rows_here, tail_rows
    )
    grad_neighbours = grads[:, None]
    return (output, grad_hidden, grad_neighbours)


def solution(mesh):
    return jax.shard_map(
        per_device,
        mesh=mesh,
        in_specs=(
            P("dp", "mp"),
            P("dp", "group", None),
            P("dp"),
            P(("dp", "group"), "mp"),
            P("group", "mp"),
            P("group", "mp"),
            P("group", "mp"),
            P("mp", "group"),
            P("dp", "mp"),
        ),
        out_specs=(P("dp", "mp"), P("dp", "mp"), P("dp", "group", None, "mp")),
        check_vma=False,
    )
```
